256 devices in a mesh: ctx: 32 (over y, z), ep: 8 (over x, core).
Axes of the slice: x: 4, y: 4, z: 8, core: 2. Of those that a mesh axis runs over, the one named last changes fastest.
Arguments:
- tokens: bfloat16 [98304, 2048], P(('ctx', 'ep')), may hold values from -6 to 6
- expert_ids: int32 [98304, 8], P(('ctx', 'ep')), may hold values from 0 to 127, as said below
- gate_codes: int32 [98304, 8], P(('ctx', 'ep')), may hold values from 4096 to 65536
- out_grad: bfloat16 [98304, 2048], P(('ctx', 'ep')), may hold values from -6 to 6
- expert_weights: bfloat16 [2048, 8, 3, 768], P('ctx', 'ep'), may hold values from -0.21875 to 0.21875
Outputs:
- moe_out: bfloat16 [98304, 2048], P(('ctx', 'ep'))
- input_grad: bfloat16 [98304, 2048], P(('ctx', 'ep'))
- weight_grads: float32 [2048, 8, 3, 768], P('ctx', 'ep')
The draws below stay inside these ranges and needn't reach their ends.
Inputs may be any that keep to these rules, and one draw needn't show every extreme that they name: `expert_ids`: each row names 8 different experts. Within each aligned block of 384 rows (the rows of one device), every expert below 8 is named by 1 to 24 rows, and one expert below 8, the same in every block, is named by exactly 24 rows in every block.
All inputs are finite; a program needn't handle non-finite values.
Results may differ from the reference program's by a relative error of at most 0.015.
Values may be sent and summed in bfloat16 or wider, within the bound.
A program may use at most 128 MiB of HBM per device.

```python
import jax
import jax.numpy as jnp
from jax import lax

D = 2048
FF = 768
EXPERTS = 128
TOPK = 8
TOK_DEV = 384
WAVE = 8
CAP = 24
TOKENS = 98304
N_CTX = 32
N_EP = 8


def draw_expert_ids(key, part):
    blocks = TOKENS // TOK_DEV
    key_hot, key_counts, key_members, key_rest, key_order = jax.random.split(key, 5)
    hot = jax.random.randint(key_hot, (), 0, WAVE)
    counts = jax.random.randint(key_counts, (blocks, WAVE), 1, CAP + 1)
    counts = jnp.where(jnp.arange(WAVE)[None, :] == hot, CAP, counts)
    member_keys = jax.random.split(key_members, blocks * WAVE)
    ranks = jax.vmap(lambda one_key: jax.random.permutation(one_key, TOK_DEV))(member_keys)
    ranks = ranks.reshape(blocks, WAVE, TOK_DEV)
    member = jnp.transpose(ranks < counts[:, :, None], (0, 2, 1))
    rest_keys = jax.random.split(key_rest, blocks * TOK_DEV)
    others = jax.vmap(lambda one_key: jax.random.permutation(one_key, EXPERTS - WAVE)[:TOPK])(rest_keys) + WAVE
    others = others.reshape(blocks, TOK_DEV, TOPK)
    wave_range = jnp.arange(WAVE)
    wave_ids = jnp.where(member, wave_range[None, None, :], EXPERTS + wave_range[None, None, :])
    joined = jnp.sort(jnp.concatenate([wave_ids, others], axis=2), axis=2)[:, :, :TOPK]
    joined = joined.reshape(TOKENS, TOPK)
    order_keys = jax.random.split(key_order, TOKENS)
    shuffled = jax.vmap(lambda one_key, row: jax.random.permutation(one_key, row))(order_keys, joined)
    return shuffled.astype(jnp.int32)


def touch_ends(result, rng, low, top_value):
    longest = result.shape.index(max(result.shape))
    spots = []
    for shift in (0, 1):
        where = [jax.random.randint(jax.random.fold_in(rng, axis), (), 0, length) for axis, length in enumerate(result.shape)]
        where[longest] = (where[longest] + shift) % result.shape[longest]
        spots.append(tuple(where))
    return result.at[spots[0]].set(low).at[spots[1]].set(top_value)


def block_scale(rng, shape, cuts, low, top_value):
    factor_of = 1.0
    for dim, blocks in cuts:
        heights = jax.random.uniform(jax.random.fold_in(jax.random.fold_in(rng, 6), dim), (blocks,), jnp.float32, low / len(cuts), top_value / len(cuts))
        factor_of = factor_of * jnp.repeat(jnp.exp(heights), shape[dim] // blocks).reshape((-1,) + (1,) * (len(shape) - 1 - dim))
    return factor_of


def gaussian(key, shape, width, most, shards=(), held_as=jnp.bfloat16):
    values = width * jax.random.normal(key, shape, jnp.float32)
    if shards:
        values = values * block_scale(key, shape, shards, -0.22, 0.18)
    return jnp.clip(values, -most, most).astype(held_as)


def setup_inputs(seed: int = 0) -> dict:
    arg_keys = jax.random.split(jax.random.key(seed), 6)
    tokens = gaussian(arg_keys[0], (TOKENS, D), 1.0, 6.0, ((0, 256),))
    expert_ids = draw_expert_ids(jax.random.fold_in(arg_keys[5], 71), 0)
    gate_codes = touch_ends(jax.random.randint(arg_keys[2], (TOKENS, TOPK), 4096, 65537), jax.random.fold_in(arg_keys[2], 1), 4096, 65536).astype(jnp.int32)
    out_grad = gaussian(arg_keys[3], (TOKENS, D), 1.0, 6.0, ((0, 256),))
    expert_weights = gaussian(arg_keys[4], (D, WAVE, 3, FF), FF ** -0.5, 0.21875, ((0, 32), (1, 8)))
    return {"tokens": tokens, "expert_ids": expert_ids, "gate_codes": gate_codes, "out_grad": out_grad, "expert_weights": expert_weights}


def reference(tokens, expert_ids, gate_codes, out_grad, expert_weights):
    blocks = TOKENS // TOK_DEV
    gates = gate_codes.astype(jnp.float32) / 65536.0
    moe = jnp.zeros((TOKENS, D), jnp.float32)
    input_grad = jnp.zeros((TOKENS, D), jnp.float32)
    tok_index = jnp.arange(TOK_DEV, dtype=jnp.int32)
    slot_index = jnp.arange(CAP, dtype=jnp.int32)
    block_start = jnp.arange(blocks, dtype=jnp.int32) * TOK_DEV
    grad_list = []
    for expert in range(WAVE):
        chosen = expert_ids == expert
        member = jnp.any(chosen, axis=1).reshape(blocks, TOK_DEV)
        weight = jnp.sum(jnp.where(chosen, gates, jnp.zeros((), gates.dtype)), axis=1)
        position = jnp.cumsum(member.astype(jnp.int32), axis=1).astype(jnp.int32) - 1
        placed = member[:, :, None] & (position[:, :, None] == slot_index[None, None, :])
        source = jnp.sum(jnp.where(placed, tok_index[None, :, None], 0), axis=1).astype(jnp.int32)
        filled = jnp.any(placed, axis=1).reshape(-1)
        flat = (source + block_start[:, None]).reshape(-1).astype(jnp.int32)
        rows_x = jnp.where(filled[:, None], tokens[flat], jnp.zeros((), tokens.dtype))
        rows_w = jnp.where(filled, weight[flat], jnp.zeros((), weight.dtype))
        route_grad = (rows_w[:, None] * out_grad[flat].astype(jnp.float32)).astype(jnp.bfloat16)
        w_gate = expert_weights[:, expert, 0, :]
        w_up = expert_weights[:, expert, 1, :]
        w_down = expert_weights[:, expert, 2, :]
        pre_gate = jnp.dot(rows_x, w_gate, preferred_element_type=jnp.float32)
        pre_up = jnp.dot(rows_x, w_up, preferred_element_type=jnp.float32)
        soft = jax.nn.sigmoid(pre_gate)
        active = pre_gate * soft
        hidden = (active * pre_up).astype(jnp.bfloat16)
        expert_out = jnp.dot(hidden, w_down.T, preferred_element_type=jnp.float32).astype(jnp.bfloat16)
        moe = moe.at[flat].add(rows_w[:, None] * expert_out.astype(jnp.float32))
        hidden_grad = jnp.dot(route_grad, w_down, preferred_element_type=jnp.float32)
        gate_grad = (hidden_grad * pre_up * soft * (1.0 + pre_gate * (1.0 - soft))).astype(jnp.bfloat16)
        up_grad = (hidden_grad * active).astype(jnp.bfloat16)
        route_input = (jnp.dot(gate_grad, w_gate.T, preferred_element_type=jnp.float32)
                       + jnp.dot(up_grad, w_up.T, preferred_element_type=jnp.float32)).astype(jnp.bfloat16)
        input_grad = input_grad.at[flat].add(route_input.astype(jnp.float32))
        group_rows = N_EP * CAP
        pieces = (rows_x.reshape(N_CTX, group_rows, D), gate_grad.reshape(N_CTX, group_rows, FF),
                  up_grad.reshape(N_CTX, group_rows, FF), route_grad.reshape(N_CTX, group_rows, D),
                  hidden.reshape(N_CTX, group_rows, FF))

        def add_group(total, piece):
            x_group, gate_group, up_group, grad_group, hidden_group = piece
            partial_sum = jnp.stack([
                jnp.dot(x_group.T, gate_group, preferred_element_type=jnp.float32),
                jnp.dot(x_group.T, up_group, preferred_element_type=jnp.float32),
                jnp.dot(grad_group.T, hidden_group, preferred_element_type=jnp.float32)], axis=1)
            return total + partial_sum.astype(jnp.bfloat16).astype(jnp.float32), None

        total, _ = lax.scan(add_group, jnp.zeros((D, 3, FF), jnp.float32), pieces)
        grad_list.append(total)
    weight_grads = jnp.stack(grad_list, axis=1)
    return moe.astype(jnp.bfloat16), input_grad.astype(jnp.bfloat16), weight_grads
```

```python
import functools

import jax
import jax.numpy as jnp
from jax import lax
from jax.experimental import pallas as pl
from jax.experimental.pallas import tpu as pltpu
from jax.sharding import PartitionSpec as P

MESH = pl.DeviceIdType.MESH
BF, F32 = jnp.bfloat16, jnp.float32
CAP = 24
PACK = 2 * CAP
LANES = 256

CUT = 112
FULL = ((0, 112), (112, 80), (112, 80))
HALF = (((0, 48), (112, 48), (112, 32)), ((48, 64), (160, 32), (144, 48)))
PLACE = (0, 112, 192)


def kernel(nx, nz, ids_ref, codes_ref, tok_hbm, og_hbm, w_hbm, moe_hbm, ig_hbm, wg_hbm,
           tok, og, wts, px, pg, pwt, slot_w, send, recv, xg, xt, pre, pre_s, pre_r,
           act, part, sum_z, sum_ya, sum_yb, back_s, back_r, moe, igr, fin_s, fin_r, wout,
           in_sem, own_s, own_r, zs, zr, yas, yar, ybs, ybr, as_, ar, es, er,
           rzs, rzr, rys, ryr, rbs, rbr, bs, br, fs, fr, out_sem):
    tokens_n = tok.shape[0]
    half_d = wts.shape[0] * 64
    ff = wts.shape[2]
    n_exp = 2 * nx
    slots = 4 * nx * CAP
    hz = nz // 2
    ctx, ep = lax.axis_index("ctx"), lax.axis_index("ep")
    y, z = lax.div(ctx, nz), lax.rem(ctx, nz)
    x, k = lax.div(ep, 2), lax.rem(ep, 2)
    h = lax.div(y, 2)
    q = lax.rem(k + h, 2)
    r = lax.rem(y + q, 2)
    other_core = (ctx, x * 2 + 1 - k)
    swap_dev = ((3 - y) * nz + z, x * 2 + 1 - k)
    y_dev = ((y + 1 - 2 * lax.rem(y, 2)) * nz + z, ep)
    z_dev = ((y * nz + lax.rem(z + 1, nz), ep), (y * nz + lax.rem(z + nz - 1, nz), ep))
    my_source = x * 4 + h * 2 + k
    my_expert = x * 2 + h

    def own(zz):
        return r * nz + lax.rem(zz + nz, nz)

    def mate(zz):
        return (1 - r) * nz + lax.rem(zz + nz, nz)

    def block(s, zz):
        return own(zz) if s < 2 else mate(zz)

    def peer(j, sign):
        dx, dh, dk = j // 4, (j // 2) % 2, j % 2
        xd = lax.rem(x + sign * dx + nx, nx)
        return xd, y + dh * (3 - 2 * y), lax.rem(h + dh, 2), lax.rem(k + dk, 2)

    def rdma(src, dst, s_sem, r_sem, dev):
        return pltpu.make_async_remote_copy(
            src_ref=src, dst_ref=dst, send_sem=s_sem, recv_sem=r_sem, device_id=dev, device_id_type=MESH
        )

    n_peer = 4 * nx
    load_tok = pltpu.make_async_copy(tok_hbm, tok, in_sem.at[0])
    load_og = pltpu.make_async_copy(og_hbm, og, in_sem.at[1])
    load_own = pltpu.make_async_copy(w_hbm, wts.at[own(z)], in_sem.at[2])
    load_tok.start()
    load_og.start()

    @pl.when(q == 0)
    def _():
        load_own.start()

    barrier = pltpu.get_barrier_semaphore()
    for j in range(1, n_peer):
        xd, yd, _, kd = peer(j, 1)
        pl.semaphore_signal(barrier, inc=1, device_id=(yd * nz + z, xd * 2 + kd), device_id_type=MESH)
    for dev in (*z_dev, y_dev):
        pl.semaphore_signal(barrier, inc=1, device_id=dev, device_id_type=MESH)
    pl.semaphore_wait(barrier, n_peer + 2)

    swap_own = rdma(w_hbm, wts.at[mate(z)], own_s, own_r, swap_dev)
    swap_in = rdma(w_hbm, wts.at[own(z)], own_s, own_r, swap_dev)

    def rows_of(d, t, s, far):
        return HALF[d][s] if t == far else FULL[s]

    def gather_z(d, t, s, arriving):
        dist = t + 1 if arriving else t
        zz = z - dist if d == 0 else z + dist
        start, count = rows_of(d, t, s, hz - 1)
        ref = wts.at[block(s, zz), pl.ds(start, count)]
        return rdma(ref, ref, zs.at[d, t, s], zr.at[d, t, s], z_dev[d])

    def gather_ya(i, arriving):
        if i == 0:
            zz, (start, count) = z, FULL[0]
        else:
            d, t = divmod(i - 1, hz)
            zz = z - 1 - t if d == 0 else z + 1 + t
            start, count = rows_of(d, t, 0, hz - 1)
        src = wts.at[mate(zz) if arriving else own(zz), pl.ds(start, count)]
        return rdma(src, src, yas.at[i], yar.at[i], y_dev)

    def gather_yb(arriving):
        ref = wts.at[mate(z) if arriving else own(z), pl.ds(*FULL[1])]
        return rdma(ref, ref, ybs, ybr, y_dev)

    def start_gather():
        for s in (0, 1):
            for d in (0, 1):
                gather_z(d, 0, s, False).start()
        gather_yb(False).start()
        gather_ya(0, False).start()

    @pl.when(q == 0)
    def _():
        load_own.wait()
        start_gather()

    @pl.when(q == 1)
    def _():
        swap_own.start()

    ids = ids_ref[...]
    gates = codes_ref[...].astype(F32) * (1.0 / 65536.0)
    member, weight = [], []
    for e in range(n_exp):
        hit = ids == e
        member.append(jnp.sum(jnp.where(hit, 1.0, 0.0), axis=0, keepdims=True))
        weight.append(jnp.sum(jnp.where(hit, gates, 0.0), axis=0, keepdims=True))
    member_all = jnp.concatenate(member, axis=0)
    before = lax.broadcasted_iota(jnp.int32, (tokens_n, tokens_n), 0)
    after = lax.broadcasted_iota(jnp.int32, (tokens_n, tokens_n), 1)
    upper = jnp.where(before <= after, 1.0, 0.0).astype(BF)
    count = jnp.dot(member_all.astype(BF), upper, preferred_element_type=F32)
    row = lax.broadcasted_iota(jnp.int32, (32, 1), 0)
    odd = k == 1
    slot_x = jnp.where(row < 16, row + 1, jnp.where(odd, jnp.where(row >= 24, row - 7, 0), jnp.where(row < 24, row + 1, 0)))
    slot_g = jnp.where(row >= 16, row - 15, jnp.where(odd, jnp.where(row < 8, row + 17, 0), jnp.where(row >= 8, row + 9, 0)))
    slot_x, slot_g = slot_x.astype(F32), slot_g.astype(F32)
    for e in range(n_exp):
        place = jnp.where(member[e] > 0.5, count[e : e + 1], -1.0)
        one_x = jnp.where(place == slot_x, 1.0, 0.0)
        one_g = jnp.where(place == slot_g, 1.0, 0.0)
        px[32 * e : 32 * e + 32, :] = one_x.astype(BF)
        pg[32 * e : 32 * e + 32, :] = one_g.astype(BF)
        slot_w[32 * e : 32 * e + 32, :] = jnp.sum(one_g * weight[e], axis=1, keepdims=True)

    @pl.when(q == 1)
    def _():
        swap_in.wait_recv()
        start_gather()

    load_tok.wait()
    load_og.wait()
    tiles = half_d // LANES

    def fill(n, carry):
        kh = lax.div(n, tiles)
        dst = pl.ds(pl.multiple_of(lax.rem(n, tiles) * LANES, LANES), LANES)
        src = pl.ds(pl.multiple_of(n * LANES, LANES), LANES)
        rows_x = jnp.dot(px[...], tok[:, src], preferred_element_type=F32)
        rows_g = jnp.dot(pg[...], og[:, src], preferred_element_type=F32) * slot_w[...]
        rows_x = rows_x.reshape(n_exp, 32, LANES)
        rows_g = rows_g.reshape(n_exp, 32, LANES)
        send[:, kh, 0:16, dst] = rows_x[:, 0:16].astype(BF)
        send[:, kh, 16:32, dst] = (rows_x[:, 16:32] + rows_g[:, 0:16]).astype(BF)
        send[:, kh, 32:48, dst] = rows_g[:, 16:32].astype(BF)
        return carry

    lax.fori_loop(0, 2 * tiles, fill, 0)

    def slots_out(j):
        xd, yd, hd, kd = peer(j, 1)
        return rdma(send.at[xd * 2 + hd, kd], recv.at[my_source], as_.at[j], ar.at[j], (yd * nz + z, xd * 2 + kd))

    def slots_in(j):
        xd, yd, hd, kd = peer(j, -1)
        ref = recv.at[xd * 4 + hd * 2 + kd]
        return rdma(ref, ref, as_.at[j], ar.at[j], (yd * nz + z, xd * 2 + kd))

    keep = pltpu.make_async_copy(send.at[my_expert, k], recv.at[my_source], as_.at[0])
    for j in range(n_peer - 1, 0, -1):
        slots_out(j).start()
    keep.start()

    for e in range(n_exp):
        at = slice(32 * e, 32 * e + 32)
        weighed = px[at, :].astype(F32) * weight[e]
        high = weighed.astype(BF).astype(F32)
        pwt[0, at, :] = high.astype(BF)
        pwt[1, at, :] = (weighed - high).astype(BF)

    gather_yb(True).wait_recv()
    for d in (0, 1):
        gather_z(d, 0, 2, False).start()

    def relay(t):
        for s in (0, 1, 2):
            for d in (0, 1):
                gather_z(d, t, s, True).wait_recv()
                if t < hz - 1:
                    gather_z(d, t + 1, s, False).start()
                if s == 0:
                    gather_ya(1 + d * hz + t, False).start()

    for t in range(hz - 1):
        relay(t)

    for j in range(1, n_peer):
        slots_in(j).wait_recv()
    keep.wait()

    def assemble(i, carry):
        at = pl.multiple_of(i * PACK, 16)
        even, uneven = recv[2 * i, 16:32, :].astype(F32), recv[2 * i + 1, 16:32, :].astype(F32)
        xg[0, pl.ds(at, 16), :] = recv[2 * i, 0:16, :]
        xg[0, pl.ds(at + 16, 16), :] = recv[2 * i + 1, 0:16, :]
        xg[0, pl.ds(at + 32, 16), :] = jnp.concatenate([even[0:8], uneven[8:16]], axis=0).astype(BF)
        xg[1, pl.ds(at, 16), :] = recv[2 * i, 32:48, :]
        xg[1, pl.ds(at + 16, 16), :] = recv[2 * i + 1, 32:48, :]
        xg[1, pl.ds(at + 32, 16), :] = jnp.concatenate([even[8:16], uneven[0:8]], axis=0).astype(BF)
        return carry

    lax.fori_loop(0, 2 * nx, assemble, 0)

    def turn(n, carry):
        at = pl.ds(pl.multiple_of(n * LANES, LANES), LANES)
        for i in (0, 1):
            xt[i, at, :] = xg[i, :, at].astype(F32).T.astype(BF)
        return carry

    lax.fori_loop(0, tiles, turn, 0)

    relay(hz - 1)
    for i in range(1 + 2 * hz):
        gather_ya(i, True).wait_recv()

    f_tiles = ff // LANES

    def swap_pre(m):
        return rdma(pre_s.at[m], pre_r.at[m], es.at[m], er.at[m], other_core)

    for m in range(3):

        def product(n, carry, m=m):
            at = pl.ds(pl.multiple_of(n * LANES, LANES), LANES)
            w = wts[:, 64 * m : 64 * m + 64, at].reshape(half_d, LANES)
            out = jnp.dot(xg[m // 2], w, preferred_element_type=F32)
            pre[m, :, at] = out
            pre_s[m, :, at] = out.astype(BF)
            return carry

        lax.fori_loop(0, f_tiles, product, 0)
        swap_pre(m).start()
    for m in range(3):
        swap_pre(m).wait_recv()

    def pointwise(n, carry):
        at = pl.ds(pl.multiple_of(n * 16, 16), 16)
        gate = pre[0, at, :] + pre_r[0, at, :].astype(F32)
        up = pre[1, at, :] + pre_r[1, at, :].astype(F32)
        grad = pre[2, at, :] + pre_r[2, at, :].astype(F32)
        soft = jax.nn.sigmoid(gate)
        active = gate * soft
        act[2, at, :] = (active * up).astype(BF)
        act[0, at, :] = (grad * up * soft * (1.0 + gate * (1.0 - soft))).astype(BF)
        act[1, at, :] = (grad * active).astype(BF)
        return carry

    lax.fori_loop(0, slots // 16, pointwise, 0)

    for m in (2, 1, 0):

        def outer(n, carry, m=m):
            at = pl.ds(pl.multiple_of(n * LANES, LANES), LANES)
            out = jnp.dot(xt[m // 2], act[m, :, at], preferred_element_type=F32)
            part[:, 64 * m : 64 * m + 64, at] = out.astype(BF).reshape(half_d // 64, 64, LANES)
            return carry

        lax.fori_loop(0, f_tiles, outer, 0)

    order = [hz] + [s * d for d in range(hz - 1, 0, -1) for s in (1, -1)] + [0]

    def reduce_ya(i):
        return rdma(part.at[mate(z + order[i]), pl.ds(0, CUT)], sum_ya.at[i], rys.at[i], ryr.at[i], y_dev)

    def reduce_z(d, t, s):
        zz = z + hz - t if d == 0 else z - hz + t
        start, count = rows_of(d, t, s, 0)
        place = PLACE[s] + start - FULL[s][0]
        return rdma(
            part.at[block(s, zz), pl.ds(start, count)],
            sum_z.at[d, t, pl.ds(place, count)],
            rzs.at[d, t, s],
            rzr.at[d, t, s],
            z_dev[d],
        )

    def add_rows(dst, src, count):
        def step(n, carry):
            at = pl.ds(pl.multiple_of(n * 16, 16), 16)
            dst[at, :] = (dst[at, :].astype(F32) + src[at, :].astype(F32)).astype(BF)
            return carry

        lax.fori_loop(0, count // 16, step, 0)

    def add_ya(i):
        reduce_ya(i).wait_recv()
        add_rows(part.at[own(z + order[i]), pl.ds(0, CUT)], sum_ya.at[i], CUT)

    def add_z(d, t, s):
        reduce_z(d, t, s).wait_recv()
        zz = z + hz - t - 1 if d == 0 else z - hz + t + 1
        start, count = rows_of(d, t, s, 0)
        place = PLACE[s] + start - FULL[s][0]
        add_rows(part.at[block(s, zz), pl.ds(start, count)], sum_z.at[d, t, pl.ds(place, count)], count)

    for i in range(2 * hz):
        reduce_ya(i).start()
    for s in (1, 2):
        for d in (0, 1):
            reduce_z(d, 0, s).start()

    def outputs(n, carry):
        rows = pl.ds(pl.multiple_of(n * (LANES // 64), LANES // 64), LANES // 64)
        at = pl.ds(pl.multiple_of(n * LANES, LANES), LANES)
        nt = (((1,), (1,)), ((), ()))
        down = wts[rows, 128:192, :].reshape(LANES, ff)
        out = lax.dot_general(act[2], down, nt, preferred_element_type=F32)
        w_gate = wts[rows, 0:64, :].reshape(LANES, ff)
        w_up = wts[rows, 64:128, :].reshape(LANES, ff)
        inp = lax.dot_general(act[0], w_gate, nt, preferred_element_type=F32)
        inp = inp + lax.dot_general(act[1], w_up, nt, preferred_element_type=F32)
        out = out.reshape(2 * nx, PACK, LANES)
        inp = inp.reshape(2 * nx, PACK, LANES)
        for i in range(2 * nx):
            back_s[2 * i, 0:16, at] = out[i, 0:16].astype(BF)
            back_s[2 * i, 16:32, at] = jnp.concatenate([out[i, 32:40], inp[i, 32:40]], axis=0).astype(BF)
            back_s[2 * i, 32:48, at] = inp[i, 0:16].astype(BF)
            back_s[2 * i + 1, 0:16, at] = out[i, 16:32].astype(BF)
            back_s[2 * i + 1, 16:32, at] = jnp.concatenate([inp[i, 40:48], out[i, 40:48]], axis=0).astype(BF)
            back_s[2 * i + 1, 32:48, at] = inp[i, 16:32].astype(BF)
        return carry

    lax.fori_loop(0, tiles, outputs, 0)

    def back_out(j):
        xd, yd, hd, kd = peer(j, 1)
        return rdma(
            back_s.at[xd * 4 + hd * 2 + kd], back_r.at[my_expert, k], bs.at[j], br.at[j], (yd * nz + z, xd * 2 + kd)
        )

    def back_in(j):
        xd, yd, hd, kd = peer(j, -1)
        ref = back_r.at[xd * 2 + hd, kd]
        return rdma(ref, ref, bs.at[j], br.at[j], (yd * nz + z, xd * 2 + kd))

    stay = pltpu.make_async_copy(back_s.at[my_source], back_r.at[my_expert, k], bs.at[0])
    for j in range(n_peer - 1, 0, -1):
        back_out(j).start()
    stay.start()

    add_ya(0)
    for d in (0, 1):
        reduce_z(d, 0, 0).start()

    def pass_on(t):
        for s in (1, 2, 0):
            for d in (0, 1):
                add_z(d, t - 1, s)
                if s == 0:
                    add_ya(1 + 2 * (t - 1) + d)
                reduce_z(d, t, s).start()

    for t in range(1, hz - 1):
        pass_on(t)

    for j in range(1, n_peer):
        back_in(j).wait_recv()
    stay.wait()

    def combine(n, carry):
        kh = lax.div(n, tiles)
        src = pl.ds(pl.multiple_of(lax.rem(n, tiles) * LANES, LANES), LANES)
        dst = pl.ds(pl.multiple_of(n * LANES, LANES), LANES)
        tn = (((0,), (0,)), ((), ()))
        rows_o = back_r[:, kh, 0:32, src].reshape(32 * n_exp, LANES)
        rows_i = back_r[:, kh, 16:48, src].reshape(32 * n_exp, LANES)
        total = lax.dot_general(pwt[0], rows_o, tn, preferred_element_type=F32)
        total = total + lax.dot_general(pwt[1], rows_o, tn, preferred_element_type=F32)
        moe[:, dst] = total.astype(BF)
        igr[:, dst] = lax.dot_general(pg[...], rows_i, tn, preferred_element_type=F32).astype(BF)
        return carry

    lax.fori_loop(0, 2 * tiles, combine, 0)
    store_moe = pltpu.make_async_copy(moe, moe_hbm, out_sem.at[0])
    store_ig = pltpu.make_async_copy(igr, ig_hbm, out_sem.at[1])
    store_moe.start()
    store_ig.start()

    pass_on(hz - 1)

    last = hz - 1
    for d in (0, 1):
        add_z(d, last, 2)
    reduce_yb = rdma(part.at[mate(z), pl.ds(*FULL[1])], sum_yb, rbs, rbr, y_dev)
    reduce_yb.start()
    reduce_ya(2 * hz - 1).wait_recv()
    for s in (1, 0):
        for d in (0, 1):
            reduce_z(d, last, s).wait_recv()
    reduce_yb.wait_recv()

    def total_rows(first, count, extra, store):
        def step(n, carry):
            at = pl.ds(pl.multiple_of(first + n * 16, 16), 16)
            near = pl.ds(pl.multiple_of(n * 16, 16), 16)
            value = part[own(z), at, :].astype(F32) + sum_z[0, last, at, :].astype(F32)
            value = value + sum_z[1, last, at, :].astype(F32) + extra[near, :].astype(F32)
            store(at, value)
            return carry

        lax.fori_loop(0, count // 16, step, 0)

    def put_out(at, value):
        wout[at, :] = value

    def put_fin(at, value):
        fin_s[at, :] = value.astype(BF)

    fin = rdma(fin_s, fin_r, fs, fr, swap_dev)

    @pl.when(q == 0)
    def _():
        total_rows(CUT, 192 - CUT, sum_yb, put_out)
        total_rows(0, CUT, sum_ya.at[2 * hz - 1], put_out)

    @pl.when(q == 1)
    def _():
        total_rows(CUT, 192 - CUT, sum_yb, put_fin)
        total_rows(0, CUT, sum_ya.at[2 * hz - 1], put_fin)
        fin.start()
        fin.wait_recv()

        def widen(n, carry):
            at = pl.ds(pl.multiple_of(n * 16, 16), 16)
            wout[at, :] = fin_r[at, :].astype(F32)
            return carry

        lax.fori_loop(0, 12, widen, 0)
        fin.wait_send()
        swap_own.wait_send()

    store_w = pltpu.make_async_copy(wout, wg_hbm, out_sem.at[2])
    store_w.start()

    for t in range(hz):
        for d in (0, 1):
            for s in (0, 1, 2):
                gather_z(d, t, s, False).wait_send()
                reduce_z(d, t, s).wait_send()
    for i in range(1 + 2 * hz):
        gather_ya(i, False).wait_send()
    gather_yb(False).wait_send()
    for i in range(2 * hz):
        reduce_ya(i).wait_send()
    reduce_yb.wait_send()
    for m in range(3):
        swap_pre(m).wait_send()
    for j in range(1, n_peer):
        slots_out(j).wait_send()
        back_out(j).wait_send()
    store_moe.wait()
    store_ig.wait()
    store_w.wait()


def layer(nx, nz, tokens, expert_ids, gate_codes, out_grad, expert_weights):
    n_tok, width = tokens.shape
    rows, _, three, ff = expert_weights.shape
    n_exp, hz, half_d = 2 * nx, nz // 2, width // 2
    blocks = 2 * nz
    slots = 4 * nx * CAP
    shard = jnp.transpose(expert_weights, (1, 2, 0, 3)).reshape(three * rows, ff)
    dma = pltpu.SemaphoreType.DMA
    vmem, hbm = pl.BlockSpec(memory_space=pltpu.VMEM), pl.BlockSpec(memory_space=pl.ANY)
    moe, input_grad, grads = pl.pallas_call(
        functools.partial(kernel, nx, nz),
        out_shape=(
            jax.ShapeDtypeStruct((n_tok, width), BF),
            jax.ShapeDtypeStruct((n_tok, width), BF),
            jax.ShapeDtypeStruct((three * rows, ff), F32),
        ),
        in_specs=[vmem, vmem, hbm, hbm, hbm],
        out_specs=(hbm, hbm, hbm),
        scratch_shapes=[
            pltpu.VMEM((n_tok, width), BF),
            pltpu.VMEM((n_tok, width), BF),
            pltpu.VMEM((blocks, 192, ff), BF),
            pltpu.VMEM((32 * n_exp, n_tok), BF),
            pltpu.VMEM((32 * n_exp, n_tok), BF),
            pltpu.VMEM((2, 32 * n_exp, n_tok), BF),
            pltpu.VMEM((32 * n_exp, 1), F32),
            pltpu.VMEM((n_exp, 2, PACK, half_d), BF),
            pltpu.VMEM((4 * nx, PACK, half_d), BF),
            pltpu.VMEM((2, slots, half_d), BF),
            pltpu.VMEM((2, half_d, slots), BF),
            pltpu.VMEM((3, slots, ff), F32),
            pltpu.VMEM((3, slots, ff), BF),
            pltpu.VMEM((3, slots, ff), BF),
            pltpu.VMEM((3, slots, ff), BF),
            pltpu.VMEM((blocks, 192, ff), BF),
            pltpu.VMEM((2, hz, 272, ff), BF),
            pltpu.VMEM((2 * hz, CUT, ff), BF),
            pltpu.VMEM((192 - CUT, ff), BF),
            pltpu.VMEM((4 * nx, PACK, half_d), BF),
            pltpu.VMEM((n_exp, 2, PACK, half_d), BF),
            pltpu.VMEM((n_tok, width), BF),
            pltpu.VMEM((n_tok, width), BF),
            pltpu.VMEM((192, ff), BF),
            pltpu.VMEM((192, ff), BF),
            pltpu.VMEM((192, ff), F32),
            dma((3,)),
            dma(()),
            dma(()),
            dma((2, hz, 3)),
            dma((2, hz, 3)),
            dma((1 + 2 * hz,)),
            dma((1 + 2 * hz,)),
            dma(()),
            dma(()),
            dma((4 * nx,)),
            dma((4 * nx,)),
            dma((3,)),
            dma((3,)),
            dma((2, hz, 3)),
            dma((2, hz, 3)),
            dma((2 * hz,)),
            dma((2 * hz,)),
            dma(()),
            dma(()),
            dma((4 * nx,)),
            dma((4 * nx,)),
            dma(()),
            dma(()),
            dma((3,)),
        ],
        compiler_params=pltpu.CompilerParams(
            collective_id=0, has_side_effects=True, vmem_limit_bytes=56 * 2**20
        ),
    )(expert_ids.T, gate_codes.T, tokens, out_grad, shard)
    grads = jnp.transpose(grads.reshape(1, three, rows, ff), (2, 0, 1, 3))
    return moe, input_grad, grads


def solution(mesh):
    nx, nz = mesh.shape["ep"] // 2, mesh.shape["ctx"] // 4
    both = P(("ctx", "ep"), None)
    weights = P("ctx", "ep", None, None)
    return jax.shard_map(
        functools.partial(layer, nx, nz),
        mesh=mesh,
        in_specs=(both, both, both, both, weights),
        out_specs=(both, both, weights),
        check_vma=False,
    )
```

```python
import functools

import jax
import jax.numpy as jnp
from jax import lax
from jax.experimental import pallas as pl
from jax.experimental.pallas import tpu as pltpu
from jax.sharding import PartitionSpec as P

MESH = pl.DeviceIdType.MESH
BF, F32 = jnp.bfloat16, jnp.float32
CAP = 24
PACK = 2 * CAP
LANES = 256

CUT = 112
FULL = ((0, 112), (112, 80), (112, 80))
HALF = (((0, 48), (112, 48), (112, 32)), ((48, 64), (160, 32), (144, 48)))
PLACE = (0, 112, 192)


def kernel(nx, nz, ids_ref, codes_ref, tok_hbm, og_hbm, w_hbm, moe_hbm, ig_hbm, wg_hbm,
           tok, og, wts, px, pg, pwt, pgt, slot_w, send, recv, xg, xt, pre, pre_s, pre_r,
           act, part, sum_z, sum_ya, fin_z, fin_ya, fin_yb, fin_own, back_s, back_r, moe, igr, wout,
           in_sem, own_s, own_r, zs, zr, yas, yar, ybs, ybr, as_, ar, es, er,
           rzs, rzr, rys, ryr, rbs, rbr, bs, br, fs, fr, out_sem):
    tokens_n = tok.shape[0]
    half_d = wts.shape[0] * 64
    ff = wts.shape[2]
    n_exp = 2 * nx
    slots = 4 * nx * CAP
    hz = nz // 2
    ctx, ep = lax.axis_index("ctx"), lax.axis_index("ep")
    y, z = lax.div(ctx, nz), lax.rem(ctx, nz)
    x, k = lax.div(ep, 2), lax.rem(ep, 2)
    h = lax.div(y, 2)
    q = lax.rem(k + h, 2)
    r = lax.rem(y + q, 2)
    other_core = (ctx, x * 2 + 1 - k)
    swap_dev = ((3 - y) * nz + z, x * 2 + 1 - k)
    y_dev = ((y + 1 - 2 * lax.rem(y, 2)) * nz + z, ep)
    z_dev = ((y * nz + lax.rem(z + 1, nz), ep), (y * nz + lax.rem(z + nz - 1, nz), ep))
    my_source = x * 4 + h * 2 + k
    my_expert = x * 2 + h

    def own(zz):
        return r * nz + lax.rem(zz + nz, nz)

    def mate(zz):
        return (1 - r) * nz + lax.rem(zz + nz, nz)

    def block(s, zz):
        return own(zz) if s < 2 else mate(zz)

    def peer(j, sign):
        dx, dh, dk = j // 4, (j // 2) % 2, j % 2
        xd = lax.rem(x + sign * dx + nx, nx)
        return xd, y + dh * (3 - 2 * y), lax.rem(h + dh, 2), lax.rem(k + dk, 2)

    def rdma(src, dst, s_sem, r_sem, dev):
        return pltpu.make_async_remote_copy(
            src_ref=src, dst_ref=dst, send_sem=s_sem, recv_sem=r_sem, device_id=dev, device_id_type=MESH
        )

    n_peer = 4 * nx
    wide = 2 * ff // 3
    group = (pl.ds(0, wide), pl.ds(wide, ff - wide))
    group_tiles = ((0, wide // LANES), (wide // LANES, ff // LANES))
    far_y, far_k = y + q * (3 - 2 * y), k + q * (1 - 2 * k)
    y_mate = y + 1 - 2 * lax.rem(y, 2)
    home_dev = (far_y * nz + z, x * 2 + far_k)
    home_z = (
        (far_y * nz + lax.rem(z + 1, nz), x * 2 + far_k),
        (far_y * nz + lax.rem(z + nz - 1, nz), x * 2 + far_k),
    )
    home_y = ((y_mate + q * (3 - 2 * y_mate)) * nz + z, x * 2 + far_k)

    load_tok = pltpu.make_async_copy(tok_hbm, tok, in_sem.at[0])
    load_og = pltpu.make_async_copy(og_hbm, og, in_sem.at[1])

    def load_own(g):
        return pltpu.make_async_copy(w_hbm.at[:, group[g]], wts.at[own(z), :, group[g]], in_sem.at[2 + g])

    @pl.when(q == 0)
    def _():
        load_own(0).start()
        load_own(1).start()

    load_tok.start()
    load_og.start()

    barrier = pltpu.get_barrier_semaphore()
    for j in range(1, n_peer):
        xd, yd, _, kd = peer(j, 1)
        pl.semaphore_signal(barrier, inc=1, device_id=(yd * nz + z, xd * 2 + kd), device_id_type=MESH)
    cross = (
        ((3 - y) * nz + lax.rem(z + 1, nz), x * 2 + 1 - k),
        ((3 - y) * nz + lax.rem(z + nz - 1, nz), x * 2 + 1 - k),
        ((3 - y_mate) * nz + z, x * 2 + 1 - k),
    )
    for dev in (*z_dev, y_dev, *cross):
        pl.semaphore_signal(barrier, inc=1, device_id=dev, device_id_type=MESH)
    pl.semaphore_wait(barrier, n_peer + 5)

    def swap_own(g, arriving):
        dst = wts.at[own(z) if arriving else mate(z), :, group[g]]
        return rdma(w_hbm.at[:, group[g]], dst, own_s.at[g], own_r.at[g], swap_dev)

    def rows_of(d, t, s, far):
        return HALF[d][s] if t == far else FULL[s]

    def gather_z(g, d, t, s, arriving):
        dist = t + 1 if arriving else t
        zz = z - dist if d == 0 else z + dist
        start, count = rows_of(d, t, s, hz - 1)
        ref = wts.at[block(s, zz), pl.ds(start, count), group[g]]
        return rdma(ref, ref, zs.at[g, d, t, s], zr.at[g, d, t, s], z_dev[d])

    def gather_ya(g, i, arriving):
        if i == 0:
            zz, (start, count) = z, FULL[0]
        else:
            d, t = divmod(i - 1, hz)
            zz = z - 1 - t if d == 0 else z + 1 + t
            start, count = rows_of(d, t, 0, hz - 1)
        ref = wts.at[mate(zz) if arriving else own(zz), pl.ds(start, count), group[g]]
        return rdma(ref, ref, yas.at[g, i], yar.at[g, i], y_dev)

    def gather_yb(g, arriving):
        ref = wts.at[mate(z) if arriving else own(z), pl.ds(*FULL[1]), group[g]]
        return rdma(ref, ref, ybs.at[g], ybr.at[g], y_dev)

    def start_gather(g):
        for s in (0, 1):
            for d in (0, 1):
                gather_z(g, d, 0, s, False).start()
        gather_yb(g, False).start()
        gather_ya(g, 0, False).start()

    def start_mates(g):
        gather_yb(g, True).wait_recv()
        for d in (0, 1):
            gather_z(g, d, 0, 2, False).start()

    def relay(g, t, s):
        for d in (0, 1):
            gather_z(g, d, t, s, True).wait_recv()
            if t < hz - 1:
                gather_z(g, d, t + 1, s, False).start()
            if s == 0:
                gather_ya(g, 1 + d * hz + t, False).start()

    @pl.when(q == 0)
    def _():
        load_own(0).wait()
        start_gather(0)
        load_own(1).wait()

    @pl.when(q == 1)
    def _():
        swap_own(0, False).start()
        swap_own(1, False).start()

    ids = ids_ref[...]
    gates = codes_ref[...].astype(F32) * (1.0 / 65536.0)
    member, weight = [], []
    for e in range(n_exp):
        hit = ids == e
        member.append(jnp.sum(jnp.where(hit, 1.0, 0.0), axis=0, keepdims=True))
        weight.append(jnp.sum(jnp.where(hit, gates, 0.0), axis=0, keepdims=True))
    member_all = jnp.concatenate(member, axis=0)
    before = lax.broadcasted_iota(jnp.int32, (tokens_n, tokens_n), 0)
    after = lax.broadcasted_iota(jnp.int32, (tokens_n, tokens_n), 1)
    upper = jnp.where(before <= after, 1.0, 0.0).astype(BF)
    count = jnp.dot(member_all.astype(BF), upper, preferred_element_type=F32)
    row = lax.broadcasted_iota(jnp.int32, (32, 1), 0)
    odd = k == 1
    slot_x = jnp.where(row < 16, row + 1, jnp.where(odd, jnp.where(row >= 24, row - 7, 0), jnp.where(row < 24, row + 1, 0)))
    slot_g = jnp.where(row >= 16, row - 15, jnp.where(odd, jnp.where(row < 8, row + 17, 0), jnp.where(row >= 8, row + 9, 0)))
    slot_x, slot_g = slot_x.astype(F32), slot_g.astype(F32)
    for e in range(n_exp):
        place = jnp.where(member[e] > 0.5, count[e : e + 1], -1.0)
        one_x = jnp.where(place == slot_x, 1.0, 0.0)
        one_g = jnp.where(place == slot_g, 1.0, 0.0)
        px[32 * e : 32 * e + 32, :] = one_x.astype(BF)
        pg[32 * e : 32 * e + 32, :] = one_g.astype(BF)
        slot_w[32 * e : 32 * e + 32, :] = jnp.sum(one_g * weight[e], axis=1, keepdims=True)

    @pl.when(q == 1)
    def _():
        swap_own(0, True).wait_recv()
        start_gather(0)

    load_tok.wait()
    load_og.wait()
    tiles = half_d // LANES

    def fill(n, carry):
        kh = lax.div(n, tiles)
        dst = pl.ds(pl.multiple_of(lax.rem(n, tiles) * LANES, LANES), LANES)
        src = pl.ds(pl.multiple_of(n * LANES, LANES), LANES)
        rows_x = jnp.dot(px[...], tok[:, src], preferred_element_type=F32)
        rows_g = jnp.dot(pg[...], og[:, src], preferred_element_type=F32) * slot_w[...]
        rows_x = rows_x.reshape(n_exp, 32, LANES)
        rows_g = rows_g.reshape(n_exp, 32, LANES)
        send[:, kh, 0:16, dst] = rows_x[:, 0:16].astype(BF)
        send[:, kh, 16:32, dst] = (rows_x[:, 16:32] + rows_g[:, 0:16]).astype(BF)
        send[:, kh, 32:48, dst] = rows_g[:, 16:32].astype(BF)
        return carry

    lax.fori_loop(0, 2 * tiles, fill, 0)

    def slots_out(j):
        xd, yd, hd, kd = peer(j, 1)
        return rdma(send.at[xd * 2 + hd, kd], recv.at[my_source], as_.at[j], ar.at[j], (yd * nz + z, xd * 2 + kd))

    def slots_in(j):
        xd, yd, hd, kd = peer(j, -1)
        ref = recv.at[xd * 4 + hd * 2 + kd]
        return rdma(ref, ref, as_.at[j], ar.at[j], (yd * nz + z, xd * 2 + kd))

    keep = pltpu.make_async_copy(send.at[my_expert, k], recv.at[my_source], as_.at[0])
    for j in range(n_peer - 1, 0, -1):
        slots_out(j).start()
    keep.start()

    start_mates(0)

    for e in range(0, n_exp, 4):
        weighed = jnp.concatenate(
            [px[32 * i : 32 * i + 32, :].astype(F32) * weight[i] for i in range(e, min(e + 4, n_exp))], axis=0
        )
        at = slice(32 * e, 32 * e + weighed.shape[0])
        weighed = weighed.T
        high = weighed.astype(BF)
        pwt[0, :, at] = high
        pwt[1, :, at] = (weighed - high.astype(F32)).astype(BF)
        pgt[:, at] = pg[at, :].astype(F32).T.astype(BF)

    def assemble(i, carry):
        at = pl.multiple_of(i * PACK, 16)
        even, uneven = recv[2 * i, 16:32, :].astype(F32), recv[2 * i + 1, 16:32, :].astype(F32)
        xg[0, pl.ds(at, 16), :] = recv[2 * i, 0:16, :]
        xg[0, pl.ds(at + 16, 16), :] = recv[2 * i + 1, 0:16, :]
        xg[0, pl.ds(at + 32, 16), :] = jnp.concatenate([even[0:8], uneven[8:16]], axis=0).astype(BF)
        xg[1, pl.ds(at, 16), :] = recv[2 * i, 32:48, :]
        xg[1, pl.ds(at + 16, 16), :] = recv[2 * i + 1, 32:48, :]
        xg[1, pl.ds(at + 32, 16), :] = jnp.concatenate([even[8:16], uneven[0:8]], axis=0).astype(BF)
        return carry

    def turn(first, end):
        def step(n, carry):
            at = pl.ds(pl.multiple_of(n * LANES, LANES), LANES)
            for i in (0, 1):
                xt[i, at, :] = xg[i, :, at].astype(F32).T.astype(BF)
            return carry

        lax.fori_loop(first, end, step, 0)

    def swap_pre(g, m):
        return rdma(
            pre_s.at[m, :, group[g]], pre_r.at[m, :, group[g]], es.at[g, m], er.at[g, m], other_core
        )

    def product(g, m):
        def step(n, carry):
            at = pl.ds(pl.multiple_of(n * LANES, LANES), LANES)
            w = wts[:, 64 * m : 64 * m + 64, at].reshape(half_d, LANES)
            out = jnp.dot(xg[m // 2], w, preferred_element_type=F32)
            pre[m, :, at] = out
            pre_s[m, :, at] = out.astype(BF)
            return carry

        lax.fori_loop(*group_tiles[g], step, 0)
        swap_pre(g, m).start()

    def pointwise(g):
        for m in range(3):
            swap_pre(g, m).wait_recv()

        def step(n, carry):
            at = pl.ds(pl.multiple_of(n * 16, 16), 16)
            gate = pre[0, at, group[g]] + pre_r[0, at, group[g]].astype(F32)
            up = pre[1, at, group[g]] + pre_r[1, at, group[g]].astype(F32)
            grad = pre[2, at, group[g]] + pre_r[2, at, group[g]].astype(F32)
            soft = jax.nn.sigmoid(gate)
            active = gate * soft
            act[2, at, group[g]] = (active * up).astype(BF)
            act[0, at, group[g]] = (grad * up * soft * (1.0 + gate * (1.0 - soft))).astype(BF)
            act[1, at, group[g]] = (grad * active).astype(BF)
            return carry

        lax.fori_loop(0, slots // 16, step, 0)

    def outer(g, m):
        def step(n, carry):
            at = pl.ds(pl.multiple_of(n * LANES, LANES), LANES)
            out = jnp.dot(xt[m // 2], act[m, :, at], preferred_element_type=F32)
            part[:, 64 * m : 64 * m + 64, at] = out.astype(BF).reshape(half_d // 64, 64, LANES)
            return carry

        lax.fori_loop(*group_tiles[g], step, 0)

    order = [hz] + [s * d for d in range(hz - 1, 0, -1) for s in (1, -1)] + [0]
    last = hz - 1

    def reduce_ya(g, i):
        src = part.at[mate(z + order[i]), pl.ds(0, CUT), group[g]]
        if order[i] == 0:
            return rdma(src, fin_ya.at[:, group[g]], rys.at[g, i], ryr.at[g, i], home_y)
        return rdma(src, sum_ya.at[i, :, group[g]], rys.at[g, i], ryr.at[g, i], y_dev)

    def reduce_yb(g):
        return rdma(
            part.at[mate(z), pl.ds(*FULL[1]), group[g]], fin_yb.at[:, group[g]], rbs.at[g], rbr.at[g], home_y
        )

    def reduce_own(g):
        return rdma(part.at[own(z), :, group[g]], fin_own.at[:, group[g]], fs.at[g], fr.at[g], home_dev)

    def reduce_z(g, d, t, s):
        zz = z + hz - t if d == 0 else z - hz + t
        start, count = rows_of(d, t, s, 0)
        place = PLACE[s] + start - FULL[s][0]
        src = part.at[block(s, zz), pl.ds(start, count), group[g]]
        if t == last and s < 2:
            dst, dev = fin_z.at[d, pl.ds(start, count), group[g]], home_z[d]
        else:
            dst, dev = sum_z.at[d, t, pl.ds(place, count), group[g]], z_dev[d]
        return rdma(src, dst, rzs.at[g, d, t, s], rzr.at[g, d, t, s], dev)

    def add_rows(dst, src, count, g):
        dst[:, group[g]] = dst[:, group[g]] + src[:, group[g]]

    def add_ya(g, i):
        reduce_ya(g, i).wait_recv()
        add_rows(part.at[own(z + order[i]), pl.ds(0, CUT)], sum_ya.at[i], CUT, g)

    def add_z(g, d, t, s):
        reduce_z(g, d, t, s).wait_recv()
        zz = z + hz - t - 1 if d == 0 else z - hz + t + 1
        start, count = rows_of(d, t, s, 0)
        place = PLACE[s] + start - FULL[s][0]
        add_rows(part.at[block(s, zz), pl.ds(start, count)], sum_z.at[d, t, pl.ds(place, count)], count, g)

    def start_reduce(g):
        for i in range(2 * hz):
            reduce_ya(g, i).start()
        for s in (1, 2):
            for d in (0, 1):
                reduce_z(g, d, 0, s).start()

        @pl.when(q == 1)
        def _():
            reduce_own(g).start()

    def start_far(g):
        add_ya(g, 0)
        for d in (0, 1):
            reduce_z(g, d, 0, 0).start()

    def pass_on(g, t, s):
        for d in (0, 1):
            add_z(g, d, t - 1, s)
            if s == 0:
                add_ya(g, 1 + 2 * (t - 1) + d)
            reduce_z(g, d, t, s).start()

    def finish_mates(g):
        for d in (0, 1):
            add_z(g, d, last, 2)
        reduce_yb(g).start()

    def finish(g):
        reduce_ya(g, 2 * hz - 1).wait_recv()
        for s in (1, 0):
            for d in (0, 1):
                reduce_z(g, d, last, s).wait_recv()
        reduce_yb(g).wait_recv()
        lane_tiles = ff // 128
        first = group_tiles[g][0] * (LANES // 128)

        def total_rows(mine, start, count, extra):
            def step(n, carry):
                at = pl.ds(pl.multiple_of(start + n * 16, 16), 16)
                near = pl.ds(pl.multiple_of(n * 16, 16), 16)
                value = mine[at, group[g]].astype(F32) + fin_z[0, at, group[g]].astype(F32)
                value = value + fin_z[1, at, group[g]].astype(F32) + extra[near, group[g]].astype(F32)
                piece = start // 16 + n
                base = lax.rem(piece, 4) * 16 * 3 * lane_tiles + lax.div(piece, 4) * lane_tiles
                for i in range(value.shape[1] // 128):
                    wout[pl.ds(base + first + i, 16, stride=3 * lane_tiles), :] = value[:, 128 * i : 128 * i + 128]
                return carry

            lax.fori_loop(0, count // 16, step, 0)

        @pl.when(q == 0)
        def _():
            total_rows(part.at[own(z)], CUT, 192 - CUT, fin_yb)
            total_rows(part.at[own(z)], 0, CUT, fin_ya)

        @pl.when(q == 1)
        def _():
            reduce_own(g).wait_recv()
            total_rows(fin_own, CUT, 192 - CUT, fin_yb)
            total_rows(fin_own, 0, CUT, fin_ya)

    def outputs(first, end):
        def step(n, carry):
            rows = pl.ds(pl.multiple_of(n * (LANES // 64), LANES // 64), LANES // 64)
            at = pl.ds(pl.multiple_of(n * LANES, LANES), LANES)
            nt = (((1,), (1,)), ((), ()))
            down = wts[rows, 128:192, :].reshape(LANES, ff)
            out = lax.dot_general(act[2], down, nt, preferred_element_type=F32)
            w_gate = wts[rows, 0:64, :].reshape(LANES, ff)
            w_up = wts[rows, 64:128, :].reshape(LANES, ff)
            inp = lax.dot_general(act[0], w_gate, nt, preferred_element_type=F32)
            inp = inp + lax.dot_general(act[1], w_up, nt, preferred_element_type=F32)
            out = out.reshape(2 * nx, PACK, LANES)
            inp = inp.reshape(2 * nx, PACK, LANES)
            for i in range(2 * nx):
                back_s[2 * i, 0:16, at] = out[i, 0:16].astype(BF)
                back_s[2 * i, 16:32, at] = jnp.concatenate([out[i, 32:40], inp[i, 32:40]], axis=0).astype(BF)
                back_s[2 * i, 32:48, at] = inp[i, 0:16].astype(BF)
                back_s[2 * i + 1, 0:16, at] = out[i, 16:32].astype(BF)
                back_s[2 * i + 1, 16:32, at] = jnp.concatenate([inp[i, 40:48], out[i, 40:48]], axis=0).astype(BF)
                back_s[2 * i + 1, 32:48, at] = inp[i, 16:32].astype(BF)
            return carry

        lax.fori_loop(first, end, step, 0)

    def back_out(j):
        xd, yd, hd, kd = peer(j, 1)
        return rdma(
            back_s.at[xd * 4 + hd * 2 + kd], back_r.at[my_expert, k], bs.at[j], br.at[j], (yd * nz + z, xd * 2 + kd)
        )

    def back_in(j):
        xd, yd, hd, kd = peer(j, -1)
        ref = back_r.at[xd * 2 + hd, kd]
        return rdma(ref, ref, bs.at[j], br.at[j], (yd * nz + z, xd * 2 + kd))

    stay = pltpu.make_async_copy(back_s.at[my_source], back_r.at[my_expert, k], bs.at[0])

    def combine(n, carry):
        kh = lax.div(n, tiles)
        src = pl.ds(pl.multiple_of(lax.rem(n, tiles) * LANES, LANES), LANES)
        dst = pl.ds(pl.multiple_of(n * LANES, LANES), LANES)
        rows_o = back_r[:, kh, 0:32, src].reshape(32 * n_exp, LANES)
        rows_i = back_r[:, kh, 16:48, src].reshape(32 * n_exp, LANES)
        total = jnp.dot(pwt[0], rows_o, preferred_element_type=F32)
        total = total + jnp.dot(pwt[1], rows_o, preferred_element_type=F32)
        moe[:, dst] = total.astype(BF)
        igr[:, dst] = jnp.dot(pgt[...], rows_i, preferred_element_type=F32).astype(BF)
        return carry

    for t in range(hz - 1):
        for s in (0, 1, 2):
            relay(0, t, s)

    @pl.when(q == 1)
    def _():
        swap_own(1, True).wait_recv()

    start_gather(1)
    for s in (0, 1, 2):
        relay(0, hz - 1, s)
    start_mates(1)
    for j in range(1, n_peer):
        slots_in(j).wait_recv()
    keep.wait()
    lax.fori_loop(0, 2 * nx, assemble, 0)
    for i in range(1 + 2 * hz):
        gather_ya(0, i, True).wait_recv()

    work = [functools.partial(product, 0, m) for m in range(3)]
    work += [functools.partial(turn, 0, tiles // 2), functools.partial(turn, tiles // 2, tiles)]
    work += [functools.partial(pointwise, 0)] + [functools.partial(outer, 0, m) for m in (2, 1, 0)]
    relays = [functools.partial(relay, 1, t, s) for t in range(hz) for s in (0, 1, 2)]
    while work or relays:
        if work:
            work.pop(0)()
        if relays:
            relays.pop(0)()

    start_reduce(0)
    for i in range(1 + 2 * hz):
        gather_ya(1, i, True).wait_recv()
    for m in range(3):
        product(1, m)
    start_far(0)
    pointwise(1)
    work = [functools.partial(outputs, n, n + 1) for n in range(tiles)]
    work += [lambda: [back_out(j).start() for j in range(n_peer - 1, 0, -1)] + [stay.start()]]
    work += [functools.partial(outer, 1, m) for m in (2, 1, 0)]
    sums = [functools.partial(pass_on, 0, t, s) for t in range(1, hz) for s in (1, 2, 0)]
    while work or sums:
        if sums:
            sums.pop(0)()
        if work:
            work.pop(0)()

    start_reduce(1)
    finish_mates(0)
    start_far(1)
    for t in range(1, hz):
        for s in (1, 2, 0):
            pass_on(1, t, s)
    finish_mates(1)

    for j in range(1, n_peer):
        back_in(j).wait_recv()
    stay.wait()
    lax.fori_loop(0, 2 * tiles, combine, 0)
    store_moe = pltpu.make_async_copy(moe, moe_hbm, out_sem.at[0])
    store_ig = pltpu.make_async_copy(igr, ig_hbm, out_sem.at[1])
    store_moe.start()
    store_ig.start()
    finish(0)
    finish(1)
    store_w = pltpu.make_async_copy(wout, wg_hbm, out_sem.at[2])
    store_w.start()

    for g in (0, 1):
        for t in range(hz):
            for d in (0, 1):
                for s in (0, 1, 2):
                    gather_z(g, d, t, s, False).wait_send()
                    reduce_z(g, d, t, s).wait_send()
        for i in range(1 + 2 * hz):
            gather_ya(g, i, False).wait_send()
        gather_yb(g, False).wait_send()
        for i in range(2 * hz):
            reduce_ya(g, i).wait_send()
        reduce_yb(g).wait_send()
        for m in range(3):
            swap_pre(g, m).wait_send()

    @pl.when(q == 1)
    def _():
        for g in (0, 1):
            swap_own(g, False).wait_send()
            reduce_own(g).wait_send()

    for j in range(1, n_peer):
        slots_out(j).wait_send()
        back_out(j).wait_send()
    store_moe.wait()
    store_ig.wait()
    store_w.wait()


def layer(nx, nz, tokens, expert_ids, gate_codes, out_grad, expert_weights):
    n_tok, width = tokens.shape
    rows, _, three, ff = expert_weights.shape
    n_exp, hz, half_d = 2 * nx, nz // 2, width // 2
    blocks = 2 * nz
    slots = 4 * nx * CAP
    shard = jnp.transpose(expert_weights, (1, 2, 0, 3)).reshape(three * rows, ff)
    dma = pltpu.SemaphoreType.DMA
    vmem, hbm = pl.BlockSpec(memory_space=pltpu.VMEM), pl.BlockSpec(memory_space=pl.ANY)
    moe, input_grad, grads = pl.pallas_call(
        functools.partial(kernel, nx, nz),
        out_shape=(
            jax.ShapeDtypeStruct((n_tok, width), BF),
            jax.ShapeDtypeStruct((n_tok, width), BF),
            jax.ShapeDtypeStruct((three * rows * ff // 128, 128), F32),
        ),
        in_specs=[vmem, vmem, hbm, hbm, hbm],
        out_specs=(hbm, hbm, hbm),
        scratch_shapes=[
            pltpu.VMEM((n_tok, width), BF),
            pltpu.VMEM((n_tok, width), BF),
            pltpu.VMEM((blocks, 192, ff), BF),
            pltpu.VMEM((32 * n_exp, n_tok), BF),
            pltpu.VMEM((32 * n_exp, n_tok), BF),
            pltpu.VMEM((2, n_tok, 32 * n_exp), BF),
            pltpu.VMEM((n_tok, 32 * n_exp), BF),
            pltpu.VMEM((32 * n_exp, 1), F32),
            pltpu.VMEM((n_exp, 2, PACK, half_d), BF),
            pltpu.VMEM((4 * nx, PACK, half_d), BF),
            pltpu.VMEM((2, slots, half_d), BF),
            pltpu.VMEM((2, half_d, slots), BF),
            pltpu.VMEM((3, slots, ff), F32),
            pltpu.VMEM((3, slots, ff), BF),
            pltpu.VMEM((3, slots, ff), BF),
            pltpu.VMEM((3, slots, ff), BF),
            pltpu.VMEM((blocks, 192, ff), BF),
            pltpu.VMEM((2, hz, 272, ff), BF),
            pltpu.VMEM((2 * hz, CUT, ff), BF),
            pltpu.VMEM((2, 192, ff), BF),
            pltpu.VMEM((CUT, ff), BF),
            pltpu.VMEM((192 - CUT, ff), BF),
            pltpu.VMEM((192, ff), BF),
            pltpu.VMEM((4 * nx, PACK, half_d), BF),
            pltpu.VMEM((n_exp, 2, PACK, half_d), BF),
            pltpu.VMEM((n_tok, width), BF),
            pltpu.VMEM((n_tok, width), BF),
            pltpu.VMEM((192 * ff // 128, 128), F32),
            dma((4,)),
            dma((2,)),
            dma((2,)),
            dma((2, 2, hz, 3)),
            dma((2, 2, hz, 3)),
            dma((2, 1 + 2 * hz)),
            dma((2, 1 + 2 * hz)),
            dma((2,)),
            dma((2,)),
            dma((4 * nx,)),
            dma((4 * nx,)),
            dma((2, 3)),
            dma((2, 3)),
            dma((2, 2, hz, 3)),
            dma((2, 2, hz, 3)),
            dma((2, 2 * hz)),
            dma((2, 2 * hz)),
            dma((2,)),
            dma((2,)),
            dma((4 * nx,)),
            dma((4 * nx,)),
            dma((2,)),
            dma((2,)),
            dma((3,)),
        ],
        compiler_params=pltpu.CompilerParams(
            collective_id=0, has_side_effects=True, vmem_limit_bytes=56 * 2**20
        ),
    )(expert_ids.T, gate_codes.T, tokens, out_grad, shard)
    return moe, input_grad, grads.reshape(rows, 1, three, ff)


def solution(mesh):
    nx, nz = mesh.shape["ep"] // 2, mesh.shape["ctx"] // 4
    both = P(("ctx", "ep"), None)
    weights = P("ctx", "ep", None, None)
    return jax.shard_map(
        functools.partial(layer, nx, nz),
        mesh=mesh,
        in_specs=(both, both, both, both, weights),
        out_specs=(both, both, weights),
        check_vma=False,
    )
```

```python
import functools

import jax
import jax.numpy as jnp
from jax import lax
from jax.experimental import pallas as pl
from jax.experimental.pallas import tpu as pltpu
from jax.sharding import PartitionSpec as P

MESH = pl.DeviceIdType.MESH
BF, F32 = jnp.bfloat16, jnp.float32
CAP = 24
PACK = 2 * CAP
LANES = 256

CUT = 112
FULL = ((0, 112), (112, 80), (112, 80))
HALF = (((0, 48), (112, 48), (112, 32)), ((48, 64), (160, 32), (144, 48)))
PLACE = (0, 112, 192)


def kernel(nx, nz, ids_ref, codes_ref, tok_hbm, og_hbm, w_hbm, moe, igr, wout,
           tok, og, wts, px, pg, pwt, pgt, slot_w, send, recv, xg, xt, pre, pre_s, pre_r,
           act, part, sum_z, sum_ya, fin_z, fin_ya, fin_yb, fin_own, back_s, back_r,
           in_sem, own_s, own_r, zs, zr, yas, yar, ybs, ybr, as_, ar, es, er,
           rzs, rzr, rys, ryr, rbs, rbr, bs, br, fs, fr):
    tokens_n = tok.shape[0]
    half_d = wts.shape[0] * 64
    ff = wts.shape[2]
    n_exp = 2 * nx
    slots = 4 * nx * CAP
    hz = nz // 2
    ctx, ep = lax.axis_index("ctx"), lax.axis_index("ep")
    y, z = lax.div(ctx, nz), lax.rem(ctx, nz)
    x, k = lax.div(ep, 2), lax.rem(ep, 2)
    h = lax.div(y, 2)
    q = lax.rem(k + h, 2)
    r = lax.rem(y + q, 2)
    other_core = (ctx, x * 2 + 1 - k)
    swap_dev = ((3 - y) * nz + z, x * 2 + 1 - k)
    y_dev = ((y + 1 - 2 * lax.rem(y, 2)) * nz + z, ep)
    z_dev = ((y * nz + lax.rem(z + 1, nz), ep), (y * nz + lax.rem(z + nz - 1, nz), ep))
    my_source = x * 4 + h * 2 + k
    my_expert = x * 2 + h

    def own(zz):
        return r * nz + lax.rem(zz + nz, nz)

    def mate(zz):
        return (1 - r) * nz + lax.rem(zz + nz, nz)

    def block(s, zz):
        return own(zz) if s < 2 else mate(zz)

    def peer(j, sign):
        dx, dh, dk = j // 4, (j // 2) % 2, j % 2
        xd = lax.rem(x + sign * dx + nx, nx)
        return xd, y + dh * (3 - 2 * y), lax.rem(h + dh, 2), lax.rem(k + dk, 2)

    def rdma(src, dst, s_sem, r_sem, dev):
        return pltpu.make_async_remote_copy(
            src_ref=src, dst_ref=dst, send_sem=s_sem, recv_sem=r_sem, device_id=dev, device_id_type=MESH
        )

    n_peer = 4 * nx
    wide = 2 * ff // 3
    group = (pl.ds(0, wide), pl.ds(wide, ff - wide))
    group_tiles = ((0, wide // LANES), (wide // LANES, ff // LANES))
    far_y, far_k = y + q * (3 - 2 * y), k + q * (1 - 2 * k)
    y_mate = y + 1 - 2 * lax.rem(y, 2)
    home_dev = (far_y * nz + z, x * 2 + far_k)
    home_z = (
        (far_y * nz + lax.rem(z + 1, nz), x * 2 + far_k),
        (far_y * nz + lax.rem(z + nz - 1, nz), x * 2 + far_k),
    )
    home_y = ((y_mate + q * (3 - 2 * y_mate)) * nz + z, x * 2 + far_k)

    load_tok = pltpu.make_async_copy(tok_hbm, tok, in_sem.at[0])
    load_og = pltpu.make_async_copy(og_hbm, og, in_sem.at[1])

    def load_own(g):
        return pltpu.make_async_copy(w_hbm.at[:, group[g]], wts.at[own(z), :, group[g]], in_sem.at[2 + g])

    @pl.when(q == 0)
    def _():
        load_own(0).start()
        load_own(1).start()

    load_tok.start()
    load_og.start()

    barrier = pltpu.get_barrier_semaphore()
    for j in range(1, n_peer):
        xd, yd, _, kd = peer(j, 1)
        pl.semaphore_signal(barrier, inc=1, device_id=(yd * nz + z, xd * 2 + kd), device_id_type=MESH)
    cross = (
        ((3 - y) * nz + lax.rem(z + 1, nz), x * 2 + 1 - k),
        ((3 - y) * nz + lax.rem(z + nz - 1, nz), x * 2 + 1 - k),
        ((3 - y_mate) * nz + z, x * 2 + 1 - k),
    )
    for dev in (*z_dev, y_dev, *cross):
        pl.semaphore_signal(barrier, inc=1, device_id=dev, device_id_type=MESH)
    pl.semaphore_wait(barrier, n_peer + 5)

    def swap_own(g, arriving):
        dst = wts.at[own(z) if arriving else mate(z), :, group[g]]
        return rdma(w_hbm.at[:, group[g]], dst, own_s.at[g], own_r.at[g], swap_dev)

    def rows_of(d, t, s, far):
        return HALF[d][s] if t == far else FULL[s]

    def gather_z(g, d, t, s, arriving):
        dist = t + 1 if arriving else t
        zz = z - dist if d == 0 else z + dist
        start, count = rows_of(d, t, s, hz - 1)
        ref = wts.at[block(s, zz), pl.ds(start, count), group[g]]
        return rdma(ref, ref, zs.at[g, d, t, s], zr.at[g, d, t, s], z_dev[d])

    def gather_ya(g, i, arriving):
        if i == 0:
            zz, (start, count) = z, FULL[0]
        else:
            d, t = divmod(i - 1, hz)
            zz = z - 1 - t if d == 0 else z + 1 + t
            start, count = rows_of(d, t, 0, hz - 1)
        ref = wts.at[mate(zz) if arriving else own(zz), pl.ds(start, count), group[g]]
        return rdma(ref, ref, yas.at[g, i], yar.at[g, i], y_dev)

    def gather_yb(g, arriving):
        ref = wts.at[mate(z) if arriving else own(z), pl.ds(*FULL[1]), group[g]]
        return rdma(ref, ref, ybs.at[g], ybr.at[g], y_dev)

    def start_gather(g):
        for s in (0, 1):
            for d in (0, 1):
                gather_z(g, d, 0, s, False).start()
        gather_yb(g, False).start()
        gather_ya(g, 0, False).start()

    def start_mates(g):
        gather_yb(g, True).wait_recv()
        for d in (0, 1):
            gather_z(g, d, 0, 2, False).start()

    def relay(g, t, s):
        for d in (0, 1):
            gather_z(g, d, t, s, True).wait_recv()
            if t < hz - 1:
                gather_z(g, d, t + 1, s, False).start()
            if s == 0:
                gather_ya(g, 1 + d * hz + t, False).start()

    @pl.when(q == 0)
    def _():
        load_own(0).wait()
        start_gather(0)
        load_own(1).wait()

    @pl.when(q == 1)
    def _():
        swap_own(0, False).start()
        swap_own(1, False).start()

    ids = ids_ref[...]
    gates = codes_ref[...].astype(F32) * (1.0 / 65536.0)
    member, weight = [], []
    for e in range(n_exp):
        hit = ids == e
        member.append(jnp.sum(jnp.where(hit, 1.0, 0.0), axis=0, keepdims=True))
        weight.append(jnp.sum(jnp.where(hit, gates, 0.0), axis=0, keepdims=True))
    member_all = jnp.concatenate(member, axis=0)
    before = lax.broadcasted_iota(jnp.int32, (tokens_n, tokens_n), 0)
    after = lax.broadcasted_iota(jnp.int32, (tokens_n, tokens_n), 1)
    upper = jnp.where(before <= after, 1.0, 0.0).astype(BF)
    count = jnp.dot(member_all.astype(BF), upper, preferred_element_type=F32)
    row = lax.broadcasted_iota(jnp.int32, (32, 1), 0)
    odd = k == 1
    slot_x = jnp.where(row < 16, row + 1, jnp.where(odd, jnp.where(row >= 24, row - 7, 0), jnp.where(row < 24, row + 1, 0)))
    slot_g = jnp.where(row >= 16, row - 15, jnp.where(odd, jnp.where(row < 8, row + 17, 0), jnp.where(row >= 8, row + 9, 0)))
    slot_x, slot_g = slot_x.astype(F32), slot_g.astype(F32)
    for e in range(n_exp):
        place = jnp.where(member[e] > 0.5, count[e : e + 1], -1.0)
        one_x = jnp.where(place == slot_x, 1.0, 0.0)
        one_g = jnp.where(place == slot_g, 1.0, 0.0)
        px[32 * e : 32 * e + 32, :] = one_x.astype(BF)
        pg[32 * e : 32 * e + 32, :] = one_g.astype(BF)
        slot_w[32 * e : 32 * e + 32, :] = jnp.sum(one_g * weight[e], axis=1, keepdims=True)

    @pl.when(q == 1)
    def _():
        swap_own(0, True).wait_recv()
        start_gather(0)

    load_tok.wait()
    load_og.wait()
    tiles = half_d // LANES

    def fill(n, carry):
        kh = lax.div(n, tiles)
        dst = pl.ds(pl.multiple_of(lax.rem(n, tiles) * LANES, LANES), LANES)
        src = pl.ds(pl.multiple_of(n * LANES, LANES), LANES)
        rows_x = jnp.dot(px[...], tok[:, src], preferred_element_type=F32)
        rows_g = jnp.dot(pg[...], og[:, src], preferred_element_type=F32) * slot_w[...]
        rows_x = rows_x.reshape(n_exp, 32, LANES)
        rows_g = rows_g.reshape(n_exp, 32, LANES)
        send[:, kh, 0:16, dst] = rows_x[:, 0:16].astype(BF)
        send[:, kh, 16:32, dst] = (rows_x[:, 16:32] + rows_g[:, 0:16]).astype(BF)
        send[:, kh, 32:48, dst] = rows_g[:, 16:32].astype(BF)
        return carry

    lax.fori_loop(0, 2 * tiles, fill, 0)

    def slots_out(j):
        xd, yd, hd, kd = peer(j, 1)
        return rdma(send.at[xd * 2 + hd, kd], recv.at[my_source], as_.at[j], ar.at[j], (yd * nz + z, xd * 2 + kd))

    def slots_in(j):
        xd, yd, hd, kd = peer(j, -1)
        ref = recv.at[xd * 4 + hd * 2 + kd]
        return rdma(ref, ref, as_.at[j], ar.at[j], (yd * nz + z, xd * 2 + kd))

    keep = pltpu.make_async_copy(send.at[my_expert, k], recv.at[my_source], as_.at[0])
    for j in range(n_peer - 1, 0, -1):
        slots_out(j).start()
    keep.start()

    start_mates(0)

    for e in range(0, n_exp, 4):
        weighed = jnp.concatenate(
            [px[32 * i : 32 * i + 32, :].astype(F32) * weight[i] for i in range(e, min(e + 4, n_exp))], axis=0
        )
        at = slice(32 * e, 32 * e + weighed.shape[0])
        weighed = weighed.T
        high = weighed.astype(BF)
        pwt[0, :, at] = high
        pwt[1, :, at] = (weighed - high.astype(F32)).astype(BF)
        pgt[:, at] = pg[at, :].astype(F32).T.astype(BF)

    def assemble(i, carry):
        at = pl.multiple_of(i * PACK, 16)
        even, uneven = recv[2 * i, 16:32, :].astype(F32), recv[2 * i + 1, 16:32, :].astype(F32)
        xg[0, pl.ds(at, 16), :] = recv[2 * i, 0:16, :]
        xg[0, pl.ds(at + 16, 16), :] = recv[2 * i + 1, 0:16, :]
        xg[0, pl.ds(at + 32, 16), :] = jnp.concatenate([even[0:8], uneven[8:16]], axis=0).astype(BF)
        xg[1, pl.ds(at, 16), :] = recv[2 * i, 32:48, :]
        xg[1, pl.ds(at + 16, 16), :] = recv[2 * i + 1, 32:48, :]
        xg[1, pl.ds(at + 32, 16), :] = jnp.concatenate([even[8:16], uneven[0:8]], axis=0).astype(BF)
        return carry

    def turn(first, end):
        def step(n, carry):
            at = pl.ds(pl.multiple_of(n * LANES, LANES), LANES)
            for i in (0, 1):
                xt[i, at, :] = xg[i, :, at].astype(F32).T.astype(BF)
            return carry

        lax.fori_loop(first, end, step, 0)

    def swap_pre(g, m):
        return rdma(
            pre_s.at[m, :, group[g]], pre_r.at[m, :, group[g]], es.at[g, m], er.at[g, m], other_core
        )

    def product(g, m):
        def step(n, carry):
            at = pl.ds(pl.multiple_of(n * LANES, LANES), LANES)
            w = wts[:, 64 * m : 64 * m + 64, at].reshape(half_d, LANES)
            out = jnp.dot(xg[m // 2], w, preferred_element_type=F32)
            pre[m, :, at] = out
            pre_s[m, :, at] = out.astype(BF)
            return carry

        lax.fori_loop(*group_tiles[g], step, 0)
        swap_pre(g, m).start()

    def pointwise(g):
        for m in range(3):
            swap_pre(g, m).wait_recv()

        def step(n, carry):
            at = pl.ds(pl.multiple_of(n * 16, 16), 16)
            gate = pre[0, at, group[g]] + pre_r[0, at, group[g]].astype(F32)
            up = pre[1, at, group[g]] + pre_r[1, at, group[g]].astype(F32)
            grad = pre[2, at, group[g]] + pre_r[2, at, group[g]].astype(F32)
            soft = jax.nn.sigmoid(gate)
            active = gate * soft
            act[2, at, group[g]] = (active * up).astype(BF)
            act[0, at, group[g]] = (grad * up * soft * (1.0 + gate * (1.0 - soft))).astype(BF)
            act[1, at, group[g]] = (grad * active).astype(BF)
            return carry

        lax.fori_loop(0, slots // 16, step, 0)

    def outer(g, m):
        def step(n, carry):
            at = pl.ds(pl.multiple_of(n * LANES, LANES), LANES)
            out = jnp.dot(xt[m // 2], act[m, :, at], preferred_element_type=F32)
            part[:, 64 * m : 64 * m + 64, at] = out.astype(BF).reshape(half_d // 64, 64, LANES)
            return carry

        lax.fori_loop(*group_tiles[g], step, 0)

    order = [hz] + [s * d for d in range(hz - 1, 0, -1) for s in (1, -1)] + [0]
    last = hz - 1

    def reduce_ya(g, i):
        src = part.at[mate(z + order[i]), pl.ds(0, CUT), group[g]]
        if order[i] == 0:
            return rdma(src, fin_ya.at[:, group[g]], rys.at[g, i], ryr.at[g, i], home_y)
        return rdma(src, sum_ya.at[i, :, group[g]], rys.at[g, i], ryr.at[g, i], y_dev)

    def reduce_yb(g):
        return rdma(
            part.at[mate(z), pl.ds(*FULL[1]), group[g]], fin_yb.at[:, group[g]], rbs.at[g], rbr.at[g], home_y
        )

    def reduce_own(g):
        return rdma(part.at[own(z), :, group[g]], fin_own.at[:, group[g]], fs.at[g], fr.at[g], home_dev)

    def reduce_z(g, d, t, s):
        zz = z + hz - t if d == 0 else z - hz + t
        start, count = rows_of(d, t, s, 0)
        place = PLACE[s] + start - FULL[s][0]
        src = part.at[block(s, zz), pl.ds(start, count), group[g]]
        if t == last and s < 2:
            dst, dev = fin_z.at[d, pl.ds(start, count), group[g]], home_z[d]
        else:
            dst, dev = sum_z.at[d, t, pl.ds(place, count), group[g]], z_dev[d]
        return rdma(src, dst, rzs.at[g, d, t, s], rzr.at[g, d, t, s], dev)

    def add_rows(dst, src, count, g):
        dst[:, group[g]] = dst[:, group[g]] + src[:, group[g]]

    def add_ya(g, i):
        reduce_ya(g, i).wait_recv()
        add_rows(part.at[own(z + order[i]), pl.ds(0, CUT)], sum_ya.at[i], CUT, g)

    def add_z(g, d, t, s):
        reduce_z(g, d, t, s).wait_recv()
        zz = z + hz - t - 1 if d == 0 else z - hz + t + 1
        start, count = rows_of(d, t, s, 0)
        place = PLACE[s] + start - FULL[s][0]
        add_rows(part.at[block(s, zz), pl.ds(start, count)], sum_z.at[d, t, pl.ds(place, count)], count, g)

    def start_reduce(g):
        for i in range(2 * hz):
            reduce_ya(g, i).start()
        for s in (1, 2):
            for d in (0, 1):
                reduce_z(g, d, 0, s).start()

        @pl.when(q == 1)
        def _():
            reduce_own(g).start()

    def start_far(g):
        add_ya(g, 0)
        for d in (0, 1):
            reduce_z(g, d, 0, 0).start()

    def pass_on(g, t, s):
        for d in (0, 1):
            add_z(g, d, t - 1, s)
            if s == 0:
                add_ya(g, 1 + 2 * (t - 1) + d)
            reduce_z(g, d, t, s).start()

    def finish_mates(g):
        for d in (0, 1):
            add_z(g, d, last, 2)
        reduce_yb(g).start()

    def finish(g):
        reduce_ya(g, 2 * hz - 1).wait_recv()
        for s in (1, 0):
            for d in (0, 1):
                reduce_z(g, d, last, s).wait_recv()
        reduce_yb(g).wait_recv()
        lane_tiles = ff // 128
        first = group_tiles[g][0] * (LANES // 128)

        def total_rows(mine, start, count, extra):
            def step(n, carry):
                at = pl.ds(pl.multiple_of(start + n * 16, 16), 16)
                near = pl.ds(pl.multiple_of(n * 16, 16), 16)
                value = mine[at, group[g]].astype(F32) + fin_z[0, at, group[g]].astype(F32)
                value = value + fin_z[1, at, group[g]].astype(F32) + extra[near, group[g]].astype(F32)
                piece = start // 16 + n
                base = lax.rem(piece, 4) * 16 * 3 * lane_tiles + lax.div(piece, 4) * lane_tiles
                for i in range(value.shape[1] // 128):
                    wout[pl.ds(base + first + i, 16, stride=3 * lane_tiles), :] = value[:, 128 * i : 128 * i + 128]
                return carry

            lax.fori_loop(0, count // 16, step, 0)

        @pl.when(q == 0)
        def _():
            total_rows(part.at[own(z)], CUT, 192 - CUT, fin_yb)
            total_rows(part.at[own(z)], 0, CUT, fin_ya)

        @pl.when(q == 1)
        def _():
            reduce_own(g).wait_recv()
            total_rows(fin_own, CUT, 192 - CUT, fin_yb)
            total_rows(fin_own, 0, CUT, fin_ya)

    def outputs(first, end):
        def step(n, carry):
            rows = pl.ds(pl.multiple_of(n * (LANES // 64), LANES // 64), LANES // 64)
            at = pl.ds(pl.multiple_of(n * LANES, LANES), LANES)
            nt = (((1,), (1,)), ((), ()))
            down = wts[rows, 128:192, :].reshape(LANES, ff)
            out = lax.dot_general(act[2], down, nt, preferred_element_type=F32)
            w_gate = wts[rows, 0:64, :].reshape(LANES, ff)
            w_up = wts[rows, 64:128, :].reshape(LANES, ff)
            inp = lax.dot_general(act[0], w_gate, nt, preferred_element_type=F32)
            inp = inp + lax.dot_general(act[1], w_up, nt, preferred_element_type=F32)
            out = out.reshape(2 * nx, PACK, LANES)
            inp = inp.reshape(2 * nx, PACK, LANES)
            for i in range(2 * nx):
                back_s[2 * i, 0:16, at] = out[i, 0:16].astype(BF)
                back_s[2 * i, 16:32, at] = jnp.concatenate([out[i, 32:40], inp[i, 32:40]], axis=0).astype(BF)
                back_s[2 * i, 32:48, at] = inp[i, 0:16].astype(BF)
                back_s[2 * i + 1, 0:16, at] = out[i, 16:32].astype(BF)
                back_s[2 * i + 1, 16:32, at] = jnp.concatenate([inp[i, 40:48], out[i, 40:48]], axis=0).astype(BF)
                back_s[2 * i + 1, 32:48, at] = inp[i, 16:32].astype(BF)
            return carry

        lax.fori_loop(first, end, step, 0)

    def back_out(j):
        xd, yd, hd, kd = peer(j, 1)
        return rdma(
            back_s.at[xd * 4 + hd * 2 + kd], back_r.at[my_expert, k], bs.at[j], br.at[j], (yd * nz + z, xd * 2 + kd)
        )

    def back_in(j):
        xd, yd, hd, kd = peer(j, -1)
        ref = back_r.at[xd * 2 + hd, kd]
        return rdma(ref, ref, bs.at[j], br.at[j], (yd * nz + z, xd * 2 + kd))

    stay = pltpu.make_async_copy(back_s.at[my_source], back_r.at[my_expert, k], bs.at[0])

    def combine(n, carry):
        kh = lax.div(n, tiles)
        src = pl.ds(pl.multiple_of(lax.rem(n, tiles) * LANES, LANES), LANES)
        dst = pl.ds(pl.multiple_of(n * LANES, LANES), LANES)
        rows_o = back_r[:, kh, 0:32, src].reshape(32 * n_exp, LANES)
        rows_i = back_r[:, kh, 16:48, src].reshape(32 * n_exp, LANES)
        total = jnp.dot(pwt[0], rows_o, preferred_element_type=F32)
        total = total + jnp.dot(pwt[1], rows_o, preferred_element_type=F32)
        moe[:, dst] = total.astype(BF)
        igr[:, dst] = jnp.dot(pgt[...], rows_i, preferred_element_type=F32).astype(BF)
        return carry

    for t in range(hz - 1):
        for s in (0, 1, 2):
            relay(0, t, s)

    @pl.when(q == 1)
    def _():
        swap_own(1, True).wait_recv()

    start_gather(1)
    for s in (0, 1, 2):
        relay(0, hz - 1, s)
    start_mates(1)
    for j in range(1, n_peer):
        slots_in(j).wait_recv()
    keep.wait()
    lax.fori_loop(0, 2 * nx, assemble, 0)
    for i in range(1 + 2 * hz):
        gather_ya(0, i, True).wait_recv()

    work = [functools.partial(product, 0, m) for m in range(3)]
    work += [functools.partial(turn, 0, tiles // 2), functools.partial(turn, tiles // 2, tiles)]
    work += [functools.partial(pointwise, 0)] + [functools.partial(outer, 0, m) for m in (2, 1, 0)]
    relays = [functools.partial(relay, 1, t, s) for t in range(hz) for s in (0, 1, 2)]
    while work or relays:
        if work:
            work.pop(0)()
        if relays:
            relays.pop(0)()

    start_reduce(0)
    for i in range(1 + 2 * hz):
        gather_ya(1, i, True).wait_recv()
    for m in range(3):
        product(1, m)
    pass_on(0, 1, 1)
    pass_on(0, 1, 2)
    pointwise(1)
    start_far(0)
    for m in (2, 1, 0):
        outer(1, m)
    start_reduce(1)
    outputs(0, tiles)
    for j in range(n_peer - 1, 0, -1):
        back_out(j).start()
    stay.start()
    for t in range(1, hz):
        if t + 1 < hz:
            pass_on(0, t + 1, 1)
            pass_on(0, t + 1, 2)
        pass_on(0, t, 0)
        pass_on(1, t, 1)
        pass_on(1, t, 2)
    finish_mates(0)
    start_far(1)
    for t in range(1, hz):
        if t == hz - 1:
            finish_mates(1)
        pass_on(1, t, 0)

    for j in range(1, n_peer):
        back_in(j).wait_recv()
    stay.wait()
    lax.fori_loop(0, 2 * tiles, combine, 0)
    finish(0)
    finish(1)

    for g in (0, 1):
        for t in range(hz):
            for d in (0, 1):
                for s in (0, 1, 2):
                    gather_z(g, d, t, s, False).wait_send()
                    reduce_z(g, d, t, s).wait_send()
        for i in range(1 + 2 * hz):
            gather_ya(g, i, False).wait_send()
        gather_yb(g, False).wait_send()
        for i in range(2 * hz):
            reduce_ya(g, i).wait_send()
        reduce_yb(g).wait_send()
        for m in range(3):
            swap_pre(g, m).wait_send()

    @pl.when(q == 1)
    def _():
        for g in (0, 1):
            swap_own(g, False).wait_send()
            reduce_own(g).wait_send()

    for j in range(1, n_peer):
        slots_out(j).wait_send()
        back_out(j).wait_send()


def layer(nx, nz, tokens, expert_ids, gate_codes, out_grad, expert_weights):
    n_tok, width = tokens.shape
    rows, _, three, ff = expert_weights.shape
    n_exp, hz, half_d = 2 * nx, nz // 2, width // 2
    blocks = 2 * nz
    slots = 4 * nx * CAP
    shard = jnp.transpose(expert_weights, (1, 2, 0, 3)).reshape(three * rows, ff)
    dma = pltpu.SemaphoreType.DMA
    vmem, hbm = pl.BlockSpec(memory_space=pltpu.VMEM), pl.BlockSpec(memory_space=pl.ANY)
    moe, input_grad, grads = pl.pallas_call(
        functools.partial(kernel, nx, nz),
        out_shape=(
            pltpu.VMEM((n_tok, width), BF),
            pltpu.VMEM((n_tok, width), BF),
            pltpu.VMEM((three * rows * ff // 128, 128), F32),
        ),
        in_specs=[vmem, vmem, hbm, hbm, hbm],
        out_specs=(vmem, vmem, vmem),
        scratch_shapes=[
            pltpu.VMEM((n_tok, width), BF),
            pltpu.VMEM((n_tok, width), BF),
            pltpu.VMEM((blocks, 192, ff), BF),
            pltpu.VMEM((32 * n_exp, n_tok), BF),
            pltpu.VMEM((32 * n_exp, n_tok), BF),
            pltpu.VMEM((2, n_tok, 32 * n_exp), BF),
            pltpu.VMEM((n_tok, 32 * n_exp), BF),
            pltpu.VMEM((32 * n_exp, 1), F32),
            pltpu.VMEM((n_exp, 2, PACK, half_d), BF),
            pltpu.VMEM((4 * nx, PACK, half_d), BF),
            pltpu.VMEM((2, slots, half_d), BF),
            pltpu.VMEM((2, half_d, slots), BF),
            pltpu.VMEM((3, slots, ff), F32),
            pltpu.VMEM((3, slots, ff), BF),
            pltpu.VMEM((3, slots, ff), BF),
            pltpu.VMEM((3, slots, ff), BF),
            pltpu.VMEM((blocks, 192, ff), BF),
            pltpu.VMEM((2, hz, 272, ff), BF),
            pltpu.VMEM((2 * hz, CUT, ff), BF),
            pltpu.VMEM((2, 192, ff), BF),
            pltpu.VMEM((CUT, ff), BF),
            pltpu.VMEM((192 - CUT, ff), BF),
            pltpu.VMEM((192, ff), BF),
            pltpu.VMEM((4 * nx, PACK, half_d), BF),
            pltpu.VMEM((n_exp, 2, PACK, half_d), BF),
            dma((4,)),
            dma((2,)),
            dma((2,)),
            dma((2, 2, hz, 3)),
            dma((2, 2, hz, 3)),
            dma((2, 1 + 2 * hz)),
            dma((2, 1 + 2 * hz)),
            dma((2,)),
            dma((2,)),
            dma((4 * nx,)),
            dma((4 * nx,)),
            dma((2, 3)),
            dma((2, 3)),
            dma((2, 2, hz, 3)),
            dma((2, 2, hz, 3)),
            dma((2, 2 * hz)),
            dma((2, 2 * hz)),
            dma((2,)),
            dma((2,)),
            dma((4 * nx,)),
            dma((4 * nx,)),
            dma((2,)),
            dma((2,)),

        ],
        compiler_params=pltpu.CompilerParams(
            collective_id=0, has_side_effects=True, vmem_limit_bytes=56 * 2**20
        ),
    )(expert_ids.T, gate_codes.T, tokens, out_grad, shard)
    return moe, input_grad, grads.reshape(rows, 1, three, ff)


def solution(mesh):
    nx, nz = mesh.shape["ep"] // 2, mesh.shape["ctx"] // 4
    both = P(("ctx", "ep"), None)
    weights = P("ctx", "ep", None, None)
    return jax.shard_map(
        functools.partial(layer, nx, nz),
        mesh=mesh,
        in_specs=(both, both, both, both, weights),
        out_specs=(both, both, weights),
        check_vma=False,
    )
```

```python
import functools

import jax
import jax.numpy as jnp
from jax import lax
from jax.experimental import pallas as pl
from jax.experimental.pallas import tpu as pltpu
from jax.sharding import PartitionSpec as P

MESH = pl.DeviceIdType.MESH
BF, F32 = jnp.bfloat16, jnp.float32
CAP = 24
PACK = 2 * CAP
LANES = 256

CUT = 112
FULL = ((0, 112), (112, 80), (112, 80))
HALF = (((0, 48), (112, 48), (112, 32)), ((48, 64), (160, 32), (144, 48)))
PLACE = (0, 112, 192)


def kernel(nx, nz, ids_ref, codes_ref, tok_hbm, og_hbm, w_hbm, moe, igr, wout,
           tok, og, wts, px, pg, pwt, pgt, slot_w, send, recv, xg, xt, pre, pre_s, pre_r,
           act, part, sum_z, sum_ya, fin_z, fin_ya, fin_yb, fin_own, back_s, back_r,
           in_sem, own_s, own_r, zs, zr, yas, yar, ybs, ybr, as_, ar, es, er,
           rzs, rzr, rys, ryr, rbs, rbr, bs, br, fs, fr):
    tokens_n = tok.shape[0]
    half_d = wts.shape[0] * 64
    ff = wts.shape[2]
    n_exp = 2 * nx
    slots = 4 * nx * CAP
    hz = nz // 2
    ctx, ep = lax.axis_index("ctx"), lax.axis_index("ep")
    y, z = lax.div(ctx, nz), lax.rem(ctx, nz)
    x, k = lax.div(ep, 2), lax.rem(ep, 2)
    h = lax.div(y, 2)
    q = lax.rem(k + h, 2)
    r = lax.rem(y + q, 2)
    other_core = (ctx, x * 2 + 1 - k)
    swap_dev = ((3 - y) * nz + z, x * 2 + 1 - k)
    y_dev = ((y + 1 - 2 * lax.rem(y, 2)) * nz + z, ep)
    z_dev = ((y * nz + lax.rem(z + 1, nz), ep), (y * nz + lax.rem(z + nz - 1, nz), ep))
    my_source = x * 4 + h * 2 + k
    my_expert = x * 2 + h

    def own(zz):
        return r * nz + lax.rem(zz + nz, nz)

    def mate(zz):
        return (1 - r) * nz + lax.rem(zz + nz, nz)

    def block(s, zz):
        return own(zz) if s < 2 else mate(zz)

    def peer(j, sign):
        dx, dh, dk = j // 4, (j // 2) % 2, j % 2
        xd = lax.rem(x + sign * dx + nx, nx)
        return xd, y + dh * (3 - 2 * y), lax.rem(h + dh, 2), lax.rem(k + dk, 2)

    def rdma(src, dst, s_sem, r_sem, dev):
        return pltpu.make_async_remote_copy(
            src_ref=src, dst_ref=dst, send_sem=s_sem, recv_sem=r_sem, device_id=dev, device_id_type=MESH
        )

    n_peer = 4 * nx
    wide = 2 * ff // 3
    group = (pl.ds(0, wide), pl.ds(wide, ff - wide))
    group_tiles = ((0, wide // LANES), (wide // LANES, ff // LANES))
    far_y, far_k = y + q * (3 - 2 * y), k + q * (1 - 2 * k)
    y_mate = y + 1 - 2 * lax.rem(y, 2)
    home_dev = (far_y * nz + z, x * 2 + far_k)
    home_z = (
        (far_y * nz + lax.rem(z + 1, nz), x * 2 + far_k),
        (far_y * nz + lax.rem(z + nz - 1, nz), x * 2 + far_k),
    )
    home_y = ((y_mate + q * (3 - 2 * y_mate)) * nz + z, x * 2 + far_k)

    load_tok = pltpu.make_async_copy(tok_hbm, tok, in_sem.at[0])
    load_og = pltpu.make_async_copy(og_hbm, og, in_sem.at[1])

    def load_own(g):
        return pltpu.make_async_copy(w_hbm.at[:, group[g]], wts.at[own(z), :, group[g]], in_sem.at[2 + g])

    @pl.when(q == 0)
    def _():
        load_own(0).start()
        load_own(1).start()

    load_tok.start()
    load_og.start()

    barrier = pltpu.get_barrier_semaphore()
    for j in range(1, n_peer):
        xd, yd, _, kd = peer(j, 1)
        pl.semaphore_signal(barrier, inc=1, device_id=(yd * nz + z, xd * 2 + kd), device_id_type=MESH)
    cross = (
        ((3 - y) * nz + lax.rem(z + 1, nz), x * 2 + 1 - k),
        ((3 - y) * nz + lax.rem(z + nz - 1, nz), x * 2 + 1 - k),
        ((3 - y_mate) * nz + z, x * 2 + 1 - k),
    )
    for dev in (*z_dev, y_dev, *cross):
        pl.semaphore_signal(barrier, inc=1, device_id=dev, device_id_type=MESH)
    pl.semaphore_wait(barrier, n_peer + 5)

    def swap_own(g, arriving):
        dst = wts.at[own(z) if arriving else mate(z), :, group[g]]
        return rdma(w_hbm.at[:, group[g]], dst, own_s.at[g], own_r.at[g], swap_dev)

    def rows_of(d, t, s, far):
        return HALF[d][s] if t == far else FULL[s]

    def gather_z(g, d, t, s, arriving):
        dist = t + 1 if arriving else t
        zz = z - dist if d == 0 else z + dist
        start, count = rows_of(d, t, s, hz - 1)
        ref = wts.at[block(s, zz), pl.ds(start, count), group[g]]
        return rdma(ref, ref, zs.at[g, d, t, s], zr.at[g, d, t, s], z_dev[d])

    def gather_ya(g, i, arriving):
        if i == 0:
            zz, (start, count) = z, FULL[0]
        else:
            d, t = divmod(i - 1, hz)
            zz = z - 1 - t if d == 0 else z + 1 + t
            start, count = rows_of(d, t, 0, hz - 1)
        ref = wts.at[mate(zz) if arriving else own(zz), pl.ds(start, count), group[g]]
        return rdma(ref, ref, yas.at[g, i], yar.at[g, i], y_dev)

    def gather_yb(g, arriving):
        ref = wts.at[mate(z) if arriving else own(z), pl.ds(*FULL[1]), group[g]]
        return rdma(ref, ref, ybs.at[g], ybr.at[g], y_dev)

    def start_gather(g):
        for s in (0, 1):
            for d in (0, 1):
                gather_z(g, d, 0, s, False).start()
        gather_yb(g, False).start()
        gather_ya(g, 0, False).start()

    def start_mates(g):
        gather_yb(g, True).wait_recv()
        for d in (0, 1):
            gather_z(g, d, 0, 2, False).start()

    def relay(g, t, s):
        for d in (0, 1):
            gather_z(g, d, t, s, True).wait_recv()
            if t < hz - 1:
                gather_z(g, d, t + 1, s, False).start()
            if s == 0:
                gather_ya(g, 1 + d * hz + t, False).start()

    @pl.when(q == 0)
    def _():
        load_own(0).wait()
        start_gather(0)
        load_own(1).wait()

    @pl.when(q == 1)
    def _():
        swap_own(0, False).start()
        swap_own(1, False).start()

    ids = ids_ref[...]
    gates = codes_ref[...].astype(F32) * (1.0 / 65536.0)
    member, weight = [], []
    for e in range(n_exp):
        hit = ids == e
        member.append(jnp.sum(jnp.where(hit, 1.0, 0.0), axis=0, keepdims=True))
        weight.append(jnp.sum(jnp.where(hit, gates, 0.0), axis=0, keepdims=True))
    member_all = jnp.concatenate(member, axis=0)
    before = lax.broadcasted_iota(jnp.int32, (tokens_n, tokens_n), 0)
    after = lax.broadcasted_iota(jnp.int32, (tokens_n, tokens_n), 1)
    upper = jnp.where(before <= after, 1.0, 0.0).astype(BF)
    count = jnp.dot(member_all.astype(BF), upper, preferred_element_type=F32)
    row = lax.broadcasted_iota(jnp.int32, (32, 1), 0)
    odd = k == 1
    slot_x = jnp.where(row < 16, row + 1, jnp.where(odd, jnp.where(row >= 24, row - 7, 0), jnp.where(row < 24, row + 1, 0)))
    slot_g = jnp.where(row >= 16, row - 15, jnp.where(odd, jnp.where(row < 8, row + 17, 0), jnp.where(row >= 8, row + 9, 0)))
    slot_x, slot_g = slot_x.astype(F32), slot_g.astype(F32)
    for e in range(n_exp):
        place = jnp.where(member[e] > 0.5, count[e : e + 1], -1.0)
        one_x = jnp.where(place == slot_x, 1.0, 0.0)
        one_g = jnp.where(place == slot_g, 1.0, 0.0)
        px[32 * e : 32 * e + 32, :] = one_x.astype(BF)
        pg[32 * e : 32 * e + 32, :] = one_g.astype(BF)
        slot_w[32 * e : 32 * e + 32, :] = jnp.sum(one_g * weight[e], axis=1, keepdims=True)

    @pl.when(q == 1)
    def _():
        swap_own(0, True).wait_recv()
        start_gather(0)

    load_tok.wait()
    load_og.wait()
    tiles = half_d // LANES

    def fill(n, carry):
        kh = lax.div(n, tiles)
        dst = pl.ds(pl.multiple_of(lax.rem(n, tiles) * LANES, LANES), LANES)
        src = pl.ds(pl.multiple_of(n * LANES, LANES), LANES)
        rows_x = jnp.dot(px[...], tok[:, src], preferred_element_type=F32)
        rows_g = jnp.dot(pg[...], og[:, src], preferred_element_type=F32) * slot_w[...]
        rows_x = rows_x.reshape(n_exp, 32, LANES)
        rows_g = rows_g.reshape(n_exp, 32, LANES)
        send[:, kh, 0:16, dst] = rows_x[:, 0:16].astype(BF)
        send[:, kh, 16:32, dst] = (rows_x[:, 16:32] + rows_g[:, 0:16]).astype(BF)
        send[:, kh, 32:48, dst] = rows_g[:, 16:32].astype(BF)
        return carry

    lax.fori_loop(0, 2 * tiles, fill, 0)

    def slots_out(j):
        xd, yd, hd, kd = peer(j, 1)
        return rdma(send.at[xd * 2 + hd, kd], recv.at[my_source], as_.at[j], ar.at[j], (yd * nz + z, xd * 2 + kd))

    def slots_in(j):
        xd, yd, hd, kd = peer(j, -1)
        ref = recv.at[xd * 4 + hd * 2 + kd]
        return rdma(ref, ref, as_.at[j], ar.at[j], (yd * nz + z, xd * 2 + kd))

    keep = pltpu.make_async_copy(send.at[my_expert, k], recv.at[my_source], as_.at[0])
    for j in range(n_peer - 1, 0, -1):
        slots_out(j).start()
    keep.start()

    start_mates(0)

    for e in range(0, n_exp, 4):
        weighed = jnp.concatenate(
            [px[32 * i : 32 * i + 32, :].astype(F32) * weight[i] for i in range(e, min(e + 4, n_exp))], axis=0
        )
        at = slice(32 * e, 32 * e + weighed.shape[0])
        weighed = weighed.T
        high = weighed.astype(BF)
        pwt[0, :, at] = high
        pwt[1, :, at] = (weighed - high.astype(F32)).astype(BF)
        pgt[:, at] = pg[at, :].astype(F32).T.astype(BF)

    def assemble(i, carry):
        at = pl.multiple_of(i * PACK, 16)
        even, uneven = recv[2 * i, 16:32, :].astype(F32), recv[2 * i + 1, 16:32, :].astype(F32)
        xg[0, pl.ds(at, 16), :] = recv[2 * i, 0:16, :]
        xg[0, pl.ds(at + 16, 16), :] = recv[2 * i + 1, 0:16, :]
        xg[0, pl.ds(at + 32, 16), :] = jnp.concatenate([even[0:8], uneven[8:16]], axis=0).astype(BF)
        xg[1, pl.ds(at, 16), :] = recv[2 * i, 32:48, :]
        xg[1, pl.ds(at + 16, 16), :] = recv[2 * i + 1, 32:48, :]
        xg[1, pl.ds(at + 32, 16), :] = jnp.concatenate([even[8:16], uneven[0:8]], axis=0).astype(BF)
        return carry

    def turn(first, end):
        def step(n, carry):
            at = pl.ds(pl.multiple_of(n * LANES, LANES), LANES)
            for i in (0, 1):
                xt[i, at, :] = xg[i, :, at].astype(F32).T.astype(BF)
            return carry

        lax.fori_loop(first, end, step, 0)

    def swap_pre(g, m):
        return rdma(
            pre_s.at[m, :, group[g]], pre_r.at[m, :, group[g]], es.at[g, m], er.at[g, m], other_core
        )

    def product(g, m):
        def step(n, carry):
            at = pl.ds(pl.multiple_of(n * LANES, LANES), LANES)
            w = wts[:, 64 * m : 64 * m + 64, at].reshape(half_d, LANES)
            out = jnp.dot(xg[m // 2], w, preferred_element_type=F32)
            pre[m, :, at] = out
            pre_s[m, :, at] = out.astype(BF)
            return carry

        lax.fori_loop(*group_tiles[g], step, 0)
        swap_pre(g, m).start()

    def pointwise(g):
        for m in range(3):
            swap_pre(g, m).wait_recv()

        def step(n, carry):
            at = pl.ds(pl.multiple_of(n * 16, 16), 16)
            gate = pre[0, at, group[g]] + pre_r[0, at, group[g]].astype(F32)
            up = pre[1, at, group[g]] + pre_r[1, at, group[g]].astype(F32)
            grad = pre[2, at, group[g]] + pre_r[2, at, group[g]].astype(F32)
            soft = jax.nn.sigmoid(gate)
            active = gate * soft
            act[2, at, group[g]] = (active * up).astype(BF)
            act[0, at, group[g]] = (grad * up * soft * (1.0 + gate * (1.0 - soft))).astype(BF)
            act[1, at, group[g]] = (grad * active).astype(BF)
            return carry

        lax.fori_loop(0, slots // 16, step, 0)

    def outer(g, m):
        def step(n, carry):
            at = pl.ds(pl.multiple_of(n * LANES, LANES), LANES)
            out = jnp.dot(xt[m // 2], act[m, :, at], preferred_element_type=F32)
            part[:, 64 * m : 64 * m + 64, at] = out.astype(BF).reshape(half_d // 64, 64, LANES)
            return carry

        lax.fori_loop(*group_tiles[g], step, 0)

    order = [hz] + [s * d for d in range(hz - 1, 0, -1) for s in (1, -1)] + [0]
    last = hz - 1

    def reduce_ya(g, i):
        src = part.at[mate(z + order[i]), pl.ds(0, CUT), group[g]]
        if order[i] == 0:
            return rdma(src, fin_ya.at[:, group[g]], rys.at[g, i], ryr.at[g, i], home_y)
        return rdma(src, sum_ya.at[i, :, group[g]], rys.at[g, i], ryr.at[g, i], y_dev)

    def reduce_yb(g):
        return rdma(
            part.at[mate(z), pl.ds(*FULL[1]), group[g]], fin_yb.at[:, group[g]], rbs.at[g], rbr.at[g], home_y
        )

    def reduce_own(g):
        return rdma(part.at[own(z), :, group[g]], fin_own.at[:, group[g]], fs.at[g], fr.at[g], home_dev)

    def reduce_z(g, d, t, s):
        zz = z + hz - t if d == 0 else z - hz + t
        start, count = rows_of(d, t, s, 0)
        place = PLACE[s] + start - FULL[s][0]
        src = part.at[block(s, zz), pl.ds(start, count), group[g]]
        if t == last and s < 2:
            dst, dev = fin_z.at[d, pl.ds(start, count), group[g]], home_z[d]
        else:
            dst, dev = sum_z.at[d, t, pl.ds(place, count), group[g]], z_dev[d]
        return rdma(src, dst, rzs.at[g, d, t, s], rzr.at[g, d, t, s], dev)

    def add_rows(dst, src, count, g):
        dst[:, group[g]] = dst[:, group[g]] + src[:, group[g]]

    def add_ya(g, i):
        reduce_ya(g, i).wait_recv()
        add_rows(part.at[own(z + order[i]), pl.ds(0, CUT)], sum_ya.at[i], CUT, g)

    def add_z(g, d, t, s):
        reduce_z(g, d, t, s).wait_recv()
        zz = z + hz - t - 1 if d == 0 else z - hz + t + 1
        start, count = rows_of(d, t, s, 0)
        place = PLACE[s] + start - FULL[s][0]
        add_rows(part.at[block(s, zz), pl.ds(start, count)], sum_z.at[d, t, pl.ds(place, count)], count, g)

    def start_reduce(g):
        for i in range(2 * hz):
            reduce_ya(g, i).start()
        for s in (1, 2):
            for d in (0, 1):
                reduce_z(g, d, 0, s).start()

        @pl.when(q == 1)
        def _():
            reduce_own(g).start()

    def start_far(g):
        add_ya(g, 0)
        for d in (0, 1):
            reduce_z(g, d, 0, 0).start()

    def pass_on(g, t, s):
        for d in (0, 1):
            add_z(g, d, t - 1, s)
            if s == 0:
                add_ya(g, 1 + 2 * (t - 1) + d)
            reduce_z(g, d, t, s).start()

    def finish_mates(g):
        for d in (0, 1):
            add_z(g, d, last, 2)
        reduce_yb(g).start()

    def finish(g, s):
        for d in (0, 1):
            reduce_z(g, d, last, s).wait_recv()
        if s == 0:
            reduce_ya(g, 2 * hz - 1).wait_recv()
            start, count, extra = 0, CUT, fin_ya
        else:
            reduce_yb(g).wait_recv()
            start, count, extra = CUT, 192 - CUT, fin_yb
        lane_tiles = ff // 128
        first = group_tiles[g][0] * (LANES // 128)

        def total_rows(mine, start, count, extra):
            def step(n, carry):
                at = pl.ds(pl.multiple_of(start + n * 16, 16), 16)
                near = pl.ds(pl.multiple_of(n * 16, 16), 16)
                value = mine[at, group[g]].astype(F32) + fin_z[0, at, group[g]].astype(F32)
                value = value + fin_z[1, at, group[g]].astype(F32) + extra[near, group[g]].astype(F32)
                piece = start // 16 + n
                base = lax.rem(piece, 4) * 16 * 3 * lane_tiles + lax.div(piece, 4) * lane_tiles
                for i in range(value.shape[1] // 128):
                    wout[pl.ds(base + first + i, 16, stride=3 * lane_tiles), :] = value[:, 128 * i : 128 * i + 128]
                return carry

            lax.fori_loop(0, count // 16, step, 0)

        @pl.when(q == 0)
        def _():
            total_rows(part.at[own(z)], start, count, extra)

        @pl.when(q == 1)
        def _():
            if s == 0:
                reduce_own(g).wait_recv()
            total_rows(fin_own, start, count, extra)

    def outputs(first, end):
        def step(n, carry):
            rows = pl.ds(pl.multiple_of(n * (LANES // 64), LANES // 64), LANES // 64)
            at = pl.ds(pl.multiple_of(n * LANES, LANES), LANES)
            nt = (((1,), (1,)), ((), ()))
            down = wts[rows, 128:192, :].reshape(LANES, ff)
            out = lax.dot_general(act[2], down, nt, preferred_element_type=F32)
            w_gate = wts[rows, 0:64, :].reshape(LANES, ff)
            w_up = wts[rows, 64:128, :].reshape(LANES, ff)
            inp = lax.dot_general(act[0], w_gate, nt, preferred_element_type=F32)
            inp = inp + lax.dot_general(act[1], w_up, nt, preferred_element_type=F32)
            out = out.reshape(2 * nx, PACK, LANES)
            inp = inp.reshape(2 * nx, PACK, LANES)
            for i in range(2 * nx):
                back_s[2 * i, 0:16, at] = out[i, 0:16].astype(BF)
                back_s[2 * i, 16:32, at] = jnp.concatenate([out[i, 32:40], inp[i, 32:40]], axis=0).astype(BF)
                back_s[2 * i, 32:48, at] = inp[i, 0:16].astype(BF)
                back_s[2 * i + 1, 0:16, at] = out[i, 16:32].astype(BF)
                back_s[2 * i + 1, 16:32, at] = jnp.concatenate([inp[i, 40:48], out[i, 40:48]], axis=0).astype(BF)
                back_s[2 * i + 1, 32:48, at] = inp[i, 16:32].astype(BF)
            return carry

        lax.fori_loop(first, end, step, 0)

    def back_out(j):
        xd, yd, hd, kd = peer(j, 1)
        return rdma(
            back_s.at[xd * 4 + hd * 2 + kd], back_r.at[my_expert, k], bs.at[j], br.at[j], (yd * nz + z, xd * 2 + kd)
        )

    def back_in(j):
        xd, yd, hd, kd = peer(j, -1)
        ref = back_r.at[xd * 2 + hd, kd]
        return rdma(ref, ref, bs.at[j], br.at[j], (yd * nz + z, xd * 2 + kd))

    stay = pltpu.make_async_copy(back_s.at[my_source], back_r.at[my_expert, k], bs.at[0])

    def combine(n, carry):
        kh = lax.div(n, tiles)
        src = pl.ds(pl.multiple_of(lax.rem(n, tiles) * LANES, LANES), LANES)
        dst = pl.ds(pl.multiple_of(n * LANES, LANES), LANES)
        rows_o = back_r[:, kh, 0:32, src].reshape(32 * n_exp, LANES)
        rows_i = back_r[:, kh, 16:48, src].reshape(32 * n_exp, LANES)
        total = jnp.dot(pwt[0], rows_o, preferred_element_type=F32)
        total = total + jnp.dot(pwt[1], rows_o, preferred_element_type=F32)
        moe[:, dst] = total.astype(BF)
        igr[:, dst] = jnp.dot(pgt[...], rows_i, preferred_element_type=F32).astype(BF)
        return carry

    for t in range(hz - 1):
        for s in (0, 1, 2):
            relay(0, t, s)

    @pl.when(q == 1)
    def _():
        swap_own(1, True).wait_recv()

    start_gather(1)
    for s in (0, 1, 2):
        relay(0, hz - 1, s)
    start_mates(1)
    for j in range(1, n_peer):
        slots_in(j).wait_recv()
    keep.wait()
    lax.fori_loop(0, 2 * nx, assemble, 0)
    for i in range(1 + 2 * hz):
        gather_ya(0, i, True).wait_recv()

    work = [functools.partial(product, 0, m) for m in range(3)]
    work += [functools.partial(turn, 0, tiles // 2), functools.partial(turn, tiles // 2, tiles)]
    work += [functools.partial(pointwise, 0)] + [functools.partial(outer, 0, m) for m in (2, 1, 0)]
    relays = [functools.partial(relay, 1, t, s) for t in range(hz) for s in (0, 1, 2)]
    while work or relays:
        if work:
            work.pop(0)()
        if relays:
            relays.pop(0)()

    start_reduce(0)
    for i in range(1 + 2 * hz):
        gather_ya(1, i, True).wait_recv()
    for m in range(3):
        product(1, m)
    pass_on(0, 1, 1)
    pass_on(0, 1, 2)
    pointwise(1)
    start_far(0)
    for m in (2, 1, 0):
        outer(1, m)
    start_reduce(1)
    outputs(0, tiles)
    for j in range(n_peer - 1, 0, -1):
        back_out(j).start()
    stay.start()
    for t in range(1, hz):
        if t + 1 < hz:
            pass_on(0, t + 1, 1)
            pass_on(0, t + 1, 2)
        pass_on(0, t, 0)
        pass_on(1, t, 1)
        pass_on(1, t, 2)
    finish_mates(0)
    start_far(1)
    for t in range(1, hz):
        if t == hz - 1:
            finish_mates(1)
        pass_on(1, t, 0)
    finish(0, 0)

    for j in range(1, n_peer):
        back_in(j).wait_recv()
    stay.wait()
    lax.fori_loop(0, 2 * tiles, combine, 0)
    finish(0, 1)
    finish(1, 0)
    finish(1, 1)

    for g in (0, 1):
        for t in range(hz):
            for d in (0, 1):
                for s in (0, 1, 2):
                    gather_z(g, d, t, s, False).wait_send()
                    reduce_z(g, d, t, s).wait_send()
        for i in range(1 + 2 * hz):
            gather_ya(g, i, False).wait_send()
        gather_yb(g, False).wait_send()
        for i in range(2 * hz):
            reduce_ya(g, i).wait_send()
        reduce_yb(g).wait_send()
        for m in range(3):
            swap_pre(g, m).wait_send()

    @pl.when(q == 1)
    def _():
        for g in (0, 1):
            swap_own(g, False).wait_send()
            reduce_own(g).wait_send()

    for j in range(1, n_peer):
        slots_out(j).wait_send()
        back_out(j).wait_send()


def layer(nx, nz, tokens, expert_ids, gate_codes, out_grad, expert_weights):
    n_tok, width = tokens.shape
    rows, _, three, ff = expert_weights.shape
    n_exp, hz, half_d = 2 * nx, nz // 2, width // 2
    blocks = 2 * nz
    slots = 4 * nx * CAP
    shard = jnp.transpose(expert_weights, (1, 2, 0, 3)).reshape(three * rows, ff)
    dma = pltpu.SemaphoreType.DMA
    vmem, hbm = pl.BlockSpec(memory_space=pltpu.VMEM), pl.BlockSpec(memory_space=pl.ANY)
    moe, input_grad, grads = pl.pallas_call(
        functools.partial(kernel, nx, nz),
        out_shape=(
            pltpu.VMEM((n_tok, width), BF),
            pltpu.VMEM((n_tok, width), BF),
            pltpu.VMEM((three * rows * ff // 128, 128), F32),
        ),
        in_specs=[vmem, vmem, hbm, hbm, hbm],
        out_specs=(vmem, vmem, vmem),
        scratch_shapes=[
            pltpu.VMEM((n_tok, width), BF),
            pltpu.VMEM((n_tok, width), BF),
            pltpu.VMEM((blocks, 192, ff), BF),
            pltpu.VMEM((32 * n_exp, n_tok), BF),
            pltpu.VMEM((32 * n_exp, n_tok), BF),
            pltpu.VMEM((2, n_tok, 32 * n_exp), BF),
            pltpu.VMEM((n_tok, 32 * n_exp), BF),
            pltpu.VMEM((32 * n_exp, 1), F32),
            pltpu.VMEM((n_exp, 2, PACK, half_d), BF),
            pltpu.VMEM((4 * nx, PACK, half_d), BF),
            pltpu.VMEM((2, slots, half_d), BF),
            pltpu.VMEM((2, half_d, slots), BF),
            pltpu.VMEM((3, slots, ff), F32),
            pltpu.VMEM((3, slots, ff), BF),
            pltpu.VMEM((3, slots, ff), BF),
            pltpu.VMEM((3, slots, ff), BF),
            pltpu.VMEM((blocks, 192, ff), BF),
            pltpu.VMEM((2, hz, 272, ff), BF),
            pltpu.VMEM((2 * hz, CUT, ff), BF),
            pltpu.VMEM((2, 192, ff), BF),
            pltpu.VMEM((CUT, ff), BF),
            pltpu.VMEM((192 - CUT, ff), BF),
            pltpu.VMEM((192, ff), BF),
            pltpu.VMEM((4 * nx, PACK, half_d), BF),
            pltpu.VMEM((n_exp, 2, PACK, half_d), BF),
            dma((4,)),
            dma((2,)),
            dma((2,)),
            dma((2, 2, hz, 3)),
            dma((2, 2, hz, 3)),
            dma((2, 1 + 2 * hz)),
            dma((2, 1 + 2 * hz)),
            dma((2,)),
            dma((2,)),
            dma((4 * nx,)),
            dma((4 * nx,)),
            dma((2, 3)),
            dma((2, 3)),
            dma((2, 2, hz, 3)),
            dma((2, 2, hz, 3)),
            dma((2, 2 * hz)),
            dma((2, 2 * hz)),
            dma((2,)),
            dma((2,)),
            dma((4 * nx,)),
            dma((4 * nx,)),
            dma((2,)),
            dma((2,)),

        ],
        compiler_params=pltpu.CompilerParams(
            collective_id=0, has_side_effects=True, vmem_limit_bytes=56 * 2**20
        ),
    )(expert_ids.T, gate_codes.T, tokens, out_grad, shard)
    return moe, input_grad, grads.reshape(rows, 1, three, ff)


def solution(mesh):
    nx, nz = mesh.shape["ep"] // 2, mesh.shape["ctx"] // 4
    both = P(("ctx", "ep"), None)
    weights = P("ctx", "ep", None, None)
    return jax.shard_map(
        functools.partial(layer, nx, nz),
        mesh=mesh,
        in_specs=(both, both, both, both, weights),
        out_specs=(both, both, weights),
        check_vma=False,
    )
```
